128 devices in a mesh: ctx: 32 (over x, y, core), head: 4 (over z).
Axes of the slice: x: 4, y: 4, z: 4, core: 2. Of those that a mesh axis runs over, the one named last changes fastest.
Arguments:
- activations: bfloat16 [8192, 2048], P('ctx'), may hold values from -6 to 6
- w_q: bfloat16 [2048, 2048], P(None, 'head'), may hold values from -0.125 to 0.125
- w_k: bfloat16 [2048, 2048], P(None, 'head'), may hold values from -0.125 to 0.125
- w_v: bfloat16 [2048, 4096], P(None, 'head'), may hold values from -0.125 to 0.125
- w_z: bfloat16 [2048, 4096], P(None, 'head'), may hold values from -0.125 to 0.125
- w_a: bfloat16 [2048, 32], P(None, 'head'), may hold values from -0.125 to 0.125
- w_b: bfloat16 [2048, 32], P(None, 'head'), may hold values from -0.125 to 0.125
- conv_q: float32 [4, 2048], P(None, 'head'), may hold values from -3 to 3
- conv_k: float32 [4, 2048], P(None, 'head'), may hold values from -3 to 3
- conv_v: float32 [4, 4096], P(None, 'head'), may hold values from -3 to 3
- a_log: float32 [32], P('head'), may hold values from -9 to -3
- dt_bias: float32 [32], P('head'), may hold values from -1 to 1
- norm_gain: float32 [128], replicated, may hold values from 0.1 to 1.9
- w_o: bfloat16 [4096, 2048], P('head'), may hold values from -0.09375 to 0.09375
Outputs:
- mixed: bfloat16 [8192, 2048], P(('ctx', 'head'))
The draws below stay inside these ranges and needn't reach their ends.
All inputs are finite; a program needn't handle non-finite values.
Results may differ from the reference program's by a relative error of at most 0.014.
Values may be sent and summed in bfloat16 or wider, within the bound.
A program may use at most 192 MiB of HBM per device.

```python
import math
import jax
import jax.numpy as jnp
from jax import lax

D = 2048
HK = 16
HV = 32
DK = 128
DV = 128
KERNEL = 4
SPAN = 64
TOKENS = 8192
KEYS = 2048
VALUES = 4096


def shard_levels(rng, shape, split, least, high):
    level = 1.0
    for axis_at, shards_of in split:
        steps = jax.random.uniform(jax.random.fold_in(jax.random.fold_in(rng, 6), axis_at), (shards_of,), jnp.float32, least / len(split), high / len(split))
        level = level * jnp.repeat(jnp.exp(steps), shape[axis_at] // shards_of).reshape((-1,) + (1,) * (len(shape) - 1 - axis_at))
    return level


def gaussian(stream_key, shape, deviation, limit, shards=(), kind=jnp.bfloat16):
    loudness = shard_levels(stream_key, shape, shards, -0.22, 0.18) if shards else 1.0
    entries = jax.random.normal(stream_key, shape, jnp.float32) * deviation * loudness
    return jnp.minimum(jnp.maximum(entries, -limit), limit).astype(kind)


def setup_inputs(seed: int = 0) -> dict:
    key_list = jax.random.split(jax.random.key(seed), 15)
    return {
        "activations": gaussian(key_list[0], (TOKENS, D), 1.0, 6.0, ((0, 32),)),
        "w_q": gaussian(key_list[1], (D, KEYS), D ** -0.5, 0.125, ((1, 4),)),
        "w_k": gaussian(key_list[2], (D, KEYS), D ** -0.5, 0.125, ((1, 4),)),
        "w_v": gaussian(key_list[3], (D, VALUES), D ** -0.5, 0.125, ((1, 4),)),
        "w_z": gaussian(key_list[4], (D, VALUES), D ** -0.5, 0.125, ((1, 4),)),
        "w_a": gaussian(key_list[5], (D, HV), D ** -0.5, 0.125, ((1, 4),)),
        "w_b": gaussian(key_list[6], (D, HV), D ** -0.5, 0.125, ((1, 4),)),
        "conv_q": gaussian(key_list[7], (KERNEL, KEYS), KERNEL ** -0.5, 3.0, ((1, 4),), jnp.float32),
        "conv_k": gaussian(key_list[8], (KERNEL, KEYS), KERNEL ** -0.5, 3.0, ((1, 4),), jnp.float32),
        "conv_v": gaussian(key_list[9], (KERNEL, VALUES), KERNEL ** -0.5, 3.0, ((1, 4),), jnp.float32),
        "a_log": jnp.clip(-9.0 + 6.0 * jax.random.uniform(key_list[10], (HV,), jnp.float32) ** shard_levels(key_list[10], (HV,), ((0, 4),), -0.2, 0.2), -9.0, -3.0),
        "dt_bias": jnp.clip(jax.random.uniform(key_list[11], (HV,), jnp.float32, -1.0, 1.0) * shard_levels(key_list[11], (HV,), ((0, 4),), -0.4, 0.0), -1.0, 1.0),
        "norm_gain": jnp.clip(1.0 + 0.18 * jax.random.normal(key_list[12], (DV,), jnp.float32), 0.1, 1.9),
        "w_o": gaussian(key_list[13], (VALUES, D), VALUES ** -0.5, 0.09375, ((0, 4),)),
    }


highest = lax.Precision.HIGHEST

def causal_conv(raw, taps):
    width = taps.shape[0]
    padded = jnp.concatenate([jnp.zeros((width - 1, raw.shape[1]), jnp.float32), raw.astype(jnp.float32)], 0)
    total = jnp.zeros(raw.shape, jnp.float32)
    for shift_pos in range(width):
        total = total + taps[shift_pos] * padded[shift_pos:shift_pos + raw.shape[0]]
    return jax.nn.silu(total)

def unit_heads(feature, groups):
    shaped = feature.reshape(feature.shape[0], groups, -1)
    shaped = shaped / jnp.sqrt(lax.optimization_barrier(jnp.sum(shaped * shaped, -1, keepdims=True)) + 1e-06)
    return shaped.reshape(feature.shape)

def block_parts(query, key, value, beta, logdecay):
    extent = query.shape[-2]
    cumulative = jnp.cumsum(logdecay, -1)
    places = jnp.arange(extent)
    strict = (places[:, None] > places[None, :]).astype(jnp.float32)
    lower = places[:, None] >= places[None, :]
    spread = cumulative[..., :, None] - cumulative[..., None, :]
    factor = jnp.exp(jnp.where(lower, spread, 0.0)) * lower.astype(jnp.float32)
    keykey = jnp.einsum('...id,...jd->...ij', key, key, precision=highest)
    system = jnp.eye(extent, dtype=jnp.float32) + beta[..., :, None] * keykey * factor * strict
    scaled = (jnp.exp(cumulative) * beta)[..., None] * key
    w_part = jax.scipy.linalg.solve_triangular(system, scaled, lower=True, unit_diagonal=True)
    u_part = jax.scipy.linalg.solve_triangular(system, beta[..., None] * value, lower=True, unit_diagonal=True)
    scores = jnp.einsum('...id,...jd->...ij', query, key, precision=highest) * factor
    inside = jnp.einsum('...ij,...jd->...id', scores, u_part, precision=highest)
    effective = jnp.exp(cumulative)[..., None] * query - jnp.einsum('...ij,...jd->...id', scores, w_part, precision=highest)
    final = cumulative[..., -1:]
    carried = jnp.exp(final - cumulative)[..., None] * key
    eye_k = jnp.eye(key.shape[-1], dtype=jnp.float32)
    transition = jnp.exp(final)[..., None] * eye_k - jnp.einsum('...id,...ie->...de', carried, w_part, precision=highest)
    feed = jnp.einsum('...id,...ie->...de', carried, u_part, precision=highest)
    return (inside, effective, transition, feed)

def reference(activations, w_q, w_k, w_v, w_z, w_a, w_b, conv_q, conv_k, conv_v, a_log, dt_bias, norm_gain, w_o):
    length = activations.shape[0]
    blocks = length // SPAN
    raw_query = jnp.dot(activations.astype(jnp.float32), w_q.astype(jnp.float32), preferred_element_type=jnp.float32).astype(jnp.bfloat16)
    raw_key = jnp.dot(activations.astype(jnp.float32), w_k.astype(jnp.float32), preferred_element_type=jnp.float32).astype(jnp.bfloat16)
    raw_value = jnp.dot(activations.astype(jnp.float32), w_v.astype(jnp.float32), preferred_element_type=jnp.float32).astype(jnp.bfloat16)
    query = unit_heads(causal_conv(raw_query, conv_q), HK) / math.sqrt(DK)
    key = unit_heads(causal_conv(raw_key, conv_k), HK)
    value = causal_conv(raw_value, conv_v)
    beta = jax.nn.sigmoid(jnp.dot(activations.astype(jnp.float32), w_b.astype(jnp.float32), preferred_element_type=jnp.float32))
    rate = jnp.exp(a_log) * jax.nn.softplus(jnp.dot(activations.astype(jnp.float32), w_a.astype(jnp.float32), preferred_element_type=jnp.float32) + dt_bias)
    ratio = HV // HK

    def one_head(index):
        key_head = (index // ratio).astype(jnp.int32)
        q_head = lax.dynamic_slice_in_dim(query, key_head * DK, DK, 1).reshape(blocks, SPAN, DK)
        k_head = lax.dynamic_slice_in_dim(key, key_head * DK, DK, 1).reshape(blocks, SPAN, DK)
        v_head = lax.dynamic_slice_in_dim(value, index.astype(jnp.int32) * DV, DV, 1).reshape(blocks, SPAN, DV)
        b_head = lax.dynamic_slice_in_dim(beta, index.astype(jnp.int32), 1, 1).reshape(blocks, SPAN)
        g_head = -lax.dynamic_slice_in_dim(rate, index.astype(jnp.int32), 1, 1).reshape(blocks, SPAN)
        inside, effective, transition, feed = block_parts(q_head, k_head, v_head, b_head, g_head)

        def advance(state, pieces):
            inside_c, effect_c, transit_c, feed_c = pieces
            result = inside_c + jnp.dot(effect_c, state, precision=highest)
            return (jnp.dot(transit_c, state, precision=highest) + feed_c, result)
        start_state = jnp.zeros((DK, DV), jnp.float32)
        _, outputs = lax.scan(advance, start_state, (inside, effective, transition, feed))
        return outputs.reshape(length, DV)
    core = lax.map(one_head, jnp.arange(HV, dtype=jnp.int32))
    core = jnp.transpose(core, (1, 0, 2))
    gate = jnp.dot(activations.astype(jnp.float32), w_z.astype(jnp.float32), preferred_element_type=jnp.float32).reshape(length, HV, DV)
    normed = core / jnp.sqrt(lax.optimization_barrier(jnp.mean(core * core, -1, keepdims=True)) + 1e-06)
    gated = (normed * norm_gain * jax.nn.silu(gate)).reshape(length, HV * DV).astype(jnp.bfloat16)
    return jnp.dot(gated.astype(jnp.float32), w_o.astype(jnp.float32), preferred_element_type=jnp.float32).astype(jnp.bfloat16)
```

```python
import functools
import math

import jax
import jax.numpy as jnp
from jax import lax
from jax.experimental import pallas as pl
from jax.experimental.pallas import tpu as pltpu
from jax.sharding import PartitionSpec as P

DK = 128
DV = 128
KERNEL = 4
HALO = 8
GROUP = 8
MESH = pl.DeviceIdType.MESH
F32 = jnp.float32
BF16 = jnp.bfloat16
VMEM_LIMIT = 56 * 1024 * 1024


def dot(a, b, dims=((1,), (0,))):
    return lax.dot_general(a, b, (dims, ((), ())), preferred_element_type=F32)


NT = ((1,), (1,))
TN = ((0,), (0,))


def conv_silu(pad, taps, rows):
    total = taps[KERNEL - 1 : KERNEL] * pad[HALO : HALO + rows]
    for back in range(1, KERNEL):
        at = HALO - back
        total = total + taps[KERNEL - 1 - back : KERNEL - back] * pad[at : at + rows]
    return total / (1.0 + jnp.exp(-total))


def unit(feature, scale):
    norm = jnp.sum(feature * feature, -1, keepdims=True) + 1e-06
    return feature * (lax.rsqrt(norm) * scale)


def invert(blocks, differ):
    one = jnp.where(differ == 0, 1.0, 0.0).astype(BF16)
    size = blocks[0].shape[0]
    inverses = None
    width = 1
    while width < size:
        mask = jnp.where((differ >= width) & (differ < 2 * width), 1.0, 0.0).astype(BF16)
        lows = [block * mask for block in blocks]
        if inverses is None:
            inverses = [one - low for low in lows]
        else:
            right = [dot(low, inv).astype(BF16) for low, inv in zip(lows, inverses)]
            left = [dot(inv, r).astype(BF16) for inv, r in zip(inverses, right)]
            inverses = [inv - l for inv, l in zip(inverses, left)]
        width *= 2
    return inverses


def gdn_kernel(
    rq, rk, rv, hq, hk, hv, cq, ck, cv, beta_ref, cum_ref, cumt_ref, m_out, inside_out, eff_out, pad
):
    rows = rq.shape[0]
    half = rows // 2
    key_heads = rq.shape[1] // DK
    ratio = rv.shape[1] // rq.shape[1]

    def smooth(raw, halo, taps, at):
        pad[0:HALO] = halo[:, at : at + DK].astype(F32)
        pad[HALO:] = raw[:, at : at + DK].astype(F32)
        return conv_silu(pad, taps[:, at : at + DK], rows)

    row_at = lax.broadcasted_iota(jnp.int32, (half, half), 0)
    col_at = lax.broadcasted_iota(jnp.int32, (half, half), 1)
    differ = row_at ^ col_at
    lower = row_at >= col_at
    strict = row_at > col_at
    heads = []
    for h in range(key_heads):
        query = unit(smooth(rq, hq, cq, h * DK), 1.0 / math.sqrt(DK))
        key = unit(smooth(rk, hk, ck, h * DK), 1.0)
        qb, kb = query.astype(BF16), key.astype(BF16)
        kk11 = dot(kb[:half], kb[:half], NT)
        kk22 = dot(kb[half:], kb[half:], NT)
        kk21 = dot(kb[half:], kb[:half], NT)
        qk11 = dot(qb[:half], kb[:half], NT)
        qk22 = dot(qb[half:], kb[half:], NT)
        qk21 = dot(qb[half:], kb[:half], NT)
        for r in range(ratio):
            j = h * ratio + r
            value = smooth(rv, hv, cv, j * DV)
            beta = beta_ref[0, :, j : j + 1]
            cum = cum_ref[0, :, j : j + 1]
            cum_row = cumt_ref[0, j : j + 1, :]
            f11 = jnp.exp(jnp.where(lower, cum[:half] - cum_row[:, :half], -1e30))
            f22 = jnp.exp(jnp.where(lower, cum[half:] - cum_row[:, half:], -1e30))
            f21 = jnp.exp(cum[half:] - cum_row[:, :half])
            a11 = jnp.where(strict, beta[:half] * kk11 * f11, 0.0).astype(BF16)
            a22 = jnp.where(strict, beta[half:] * kk22 * f22, 0.0).astype(BF16)
            a21 = (beta[half:] * kk21 * f21).astype(BF16)
            s11 = (qk11 * f11).astype(BF16)
            s22 = (qk22 * f22).astype(BF16)
            s21 = (qk21 * f21).astype(BF16)
            grow = jnp.exp(cum)
            rhs = jnp.concatenate([key * (grow * beta), value * beta], 1)
            heads.append((j, query, kb, cum, grow, a11, a22, a21, s11, s22, s21, rhs))
    inverses = invert([a for item in heads for a in (item[5], item[6])], differ)
    eye = jnp.where(
        lax.broadcasted_iota(jnp.int32, (DK, DK), 0) == lax.broadcasted_iota(jnp.int32, (DK, DK), 1), 1.0, 0.0
    )
    for n, (j, query, kb, cum, grow, _, _, a21, s11, s22, s21, rhs) in enumerate(heads):
        wu1 = dot(inverses[2 * n], rhs[:half].astype(BF16)).astype(BF16)
        low = rhs[half:] - dot(a21, wu1)
        wu2f = dot(inverses[2 * n + 1], low.astype(BF16))
        wu2 = wu2f.astype(BF16)
        in1 = dot(s11, wu1)
        in2 = dot(s21, wu1) + dot(s22, wu2)
        inside_out[0:half, j * DV : (j + 1) * DV] = in1[:, DK:]
        inside_out[half:, j * DV : (j + 1) * DV] = in2[:, DK:]
        eff = grow * query
        eff_out[0:half, j * DK : (j + 1) * DK] = (eff[:half] - in1[:, :DK]).astype(BF16)
        eff_out[half:, j * DK : (j + 1) * DK] = (eff[half:] - in2[:, :DK]).astype(BF16)
        final = cum[rows - 1 : rows]
        carry = jnp.exp(final - cum)
        tf = dot(kb[:half], (wu1.astype(F32) * carry[:half]).astype(BF16), TN) + dot(
            kb[half:], (wu2f * carry[half:]).astype(BF16), TN
        )
        m_out[j, :, :DK] = ((jnp.exp(final) - 1.0) * eye - tf[:, :DK]).astype(BF16)
        m_out[j, :, DK:] = tf[:, DK:].astype(BF16)


def gdn(raw_q, raw_k, raw_v, halo, conv_q, conv_k, conv_v, beta, cum, steps):
    rows = raw_q.shape[0]
    heads = beta.shape[1]
    per = heads // steps
    kw, vw = raw_q.shape[1] // steps, raw_v.shape[1] // steps
    w = raw_q.shape[1]

    def cols(n, width, first=0):
        return pl.BlockSpec((n, width), lambda s: (0, s + first))

    beta3 = jnp.transpose(beta.reshape(rows, steps, per), (1, 0, 2))
    cum3 = jnp.transpose(cum.reshape(rows, steps, per), (1, 0, 2))
    cumt = jnp.transpose(cum).reshape(steps, per, rows)
    three = lambda s: (s, 0, 0)
    return pl.pallas_call(
        gdn_kernel,
        grid=(steps,),
        in_specs=[
            cols(rows, kw),
            cols(rows, kw),
            cols(rows, vw),
            cols(HALO, kw),
            cols(HALO, kw, w // kw),
            cols(HALO, vw, 2 * w // vw),
            cols(KERNEL, kw),
            cols(KERNEL, kw),
            cols(KERNEL, vw),
            pl.BlockSpec((1, rows, per), three),
            pl.BlockSpec((1, rows, per), three),
            pl.BlockSpec((1, per, rows), three),
        ],
        out_specs=[
            pl.BlockSpec((per, DK, DK + DV), three),
            cols(rows, vw),
            cols(rows, per * DK),
        ],
        out_shape=[
            jax.ShapeDtypeStruct((heads, DK, DK + DV), BF16),
            jax.ShapeDtypeStruct((rows, heads * DV), F32),
            jax.ShapeDtypeStruct((rows, heads * DK), BF16),
        ],
        scratch_shapes=[pltpu.VMEM((HALO + rows, DK), F32)],
        compiler_params=pltpu.CompilerParams(vmem_limit_bytes=VMEM_LIMIT),
        name="gdn_local",
    )(raw_q, raw_k, raw_v, halo, halo, halo, conv_q, conv_k, conv_v, beta3, cum3, cumt)


def remote(src, dst, send, recv, ctx, head):
    return pltpu.make_async_remote_copy(
        src_ref=src, dst_ref=dst, send_sem=send, recv_sem=recv, device_id=(ctx, head), device_id_type=MESH
    )


def compose(later, earlier):
    return later + earlier + dot(later[:, :DK].astype(BF16), earlier.astype(BF16))


def exchange_kernel(groups, m_ref, s_out, land, total, land2, pref, state, sbuf, send1, recv1, send2, recv2, send3, recv3):
    c = lax.axis_index("ctx")
    z = lax.axis_index("head")
    g = c // GROUP
    me = lax.rem(c, GROUP)
    base = g * GROUP

    barrier = pltpu.get_barrier_semaphore()
    for d in range(1, GROUP):
        peer = base + lax.rem(me + d, GROUP)
        pl.semaphore_signal(barrier, inc=1, device_id=(peer, z), device_id_type=MESH)
    for d in range(1, groups):
        peer = lax.rem(g + d, groups) * GROUP + me
        pl.semaphore_signal(barrier, inc=1, device_id=(peer, z), device_id_type=MESH)
    pl.semaphore_wait(barrier, GROUP - 1 + groups - 1)

    for d in range(1, GROUP):
        peer = lax.rem(me + d, GROUP)
        remote(m_ref.at[peer], land.at[me], send1.at[d], recv1.at[me], base + peer, z).start()
    land[me] = m_ref[me]
    for d in range(1, GROUP):
        peer = lax.rem(me + d, GROUP)
        remote(m_ref.at[peer], land.at[peer], send1.at[d], recv1.at[peer], base + peer, z).wait_recv()

    maps = [land[j].astype(F32) for j in range(GROUP)]
    p01 = compose(maps[1], maps[0])
    p23 = compose(maps[3], maps[2])
    p45 = compose(maps[5], maps[4])
    p67 = compose(maps[7], maps[6])
    p03 = compose(p23, p01)
    p47 = compose(p67, p45)
    whole = compose(p47, p03)
    total[...] = whole.astype(BF16)
    for other in range(1, groups):

        @pl.when(g < other)
        def _():
            remote(total, land2.at[g], send2.at[other], recv2.at[g], other * GROUP + me, z).start()

    p02 = compose(maps[2], p01)
    p04 = compose(maps[4], p03)
    p05 = compose(p45, p03)
    p06 = compose(maps[6], p05)
    for j, item in enumerate((maps[0], p01, p02, p03, p04, p05, p06)):
        pref[j] = item

    state[...] = jnp.zeros_like(state)
    for other in range(groups - 1):

        @pl.when(other < g)
        def _():
            remote(total, land2.at[other], send2.at[0], recv2.at[other], other * GROUP + me, z).wait_recv()
            now = state[...]
            step = land2[other]
            state[...] = now + step[:, DK:].astype(F32) + dot(step[:, :DK], now.astype(BF16))

    now = state[...]
    low = now.astype(BF16)
    for j in range(GROUP):
        if j == 0:
            sbuf[j] = low
        else:
            item = pref[j - 1]
            sbuf[j] = (now + item[:, DK:] + dot(item[:, :DK].astype(BF16), low)).astype(BF16)

        @pl.when(j != me)
        def _(j=j):
            remote(sbuf.at[j], s_out.at[me], send3.at[j], recv3.at[me], base + j, z).start()

    s_out[me] = sbuf[me]
    for j in range(GROUP):

        @pl.when(j != me)
        def _(j=j):
            remote(sbuf.at[j], s_out.at[j], send3.at[j], recv3.at[j], base + j, z).wait_recv()

    for d in range(1, GROUP):
        peer = lax.rem(me + d, GROUP)
        remote(m_ref.at[peer], land.at[me], send1.at[d], recv1.at[me], base + peer, z).wait_send()
    for other in range(1, groups):

        @pl.when(g < other)
        def _():
            remote(total, land2.at[g], send2.at[other], recv2.at[g], other * GROUP + me, z).wait_send()

    for j in range(GROUP):

        @pl.when(j != me)
        def _(j=j):
            remote(sbuf.at[j], s_out.at[me], send3.at[j], recv3.at[me], base + j, z).wait_send()


def exchange(maps, groups):
    heads = maps.shape[0]
    vmem = pl.BlockSpec(memory_space=pltpu.VMEM)
    return pl.pallas_call(
        functools.partial(exchange_kernel, groups),
        in_specs=[vmem],
        out_specs=vmem,
        out_shape=jax.ShapeDtypeStruct((heads, DK, DV), BF16),
        scratch_shapes=[
            pltpu.VMEM((GROUP, DK, DK + DV), BF16),
            pltpu.VMEM((DK, DK + DV), BF16),
            pltpu.VMEM((groups, DK, DK + DV), BF16),
            pltpu.VMEM((GROUP, DK, DK + DV), F32),
            pltpu.VMEM((DK, DV), F32),
            pltpu.VMEM((GROUP, DK, DV), BF16),
            pltpu.SemaphoreType.DMA((GROUP,)),
            pltpu.SemaphoreType.DMA((GROUP,)),
            pltpu.SemaphoreType.DMA((groups,)),
            pltpu.SemaphoreType.DMA((groups,)),
            pltpu.SemaphoreType.DMA((GROUP,)),
            pltpu.SemaphoreType.DMA((GROUP,)),
        ],
        compiler_params=pltpu.CompilerParams(
            collective_id=0, has_side_effects=True, vmem_limit_bytes=VMEM_LIMIT
        ),
        name="states",
    )(maps)


def finish_kernel(inside, eff, s_in, gate, gain, w_o, part, gated):
    heads = s_in.shape[0]
    for j in range(heads):
        at = slice(j * DV, (j + 1) * DV)
        core = inside[:, at] + dot(eff[:, at], s_in[j])
        scale = lax.rsqrt(jnp.mean(core * core, -1, keepdims=True) + 1e-06)
        z = gate[:, at]
        gated[:, at] = (core * scale * gain[...] * (z / (1.0 + jnp.exp(-z)))).astype(BF16)
    width = 512
    for n in range(part.shape[2] // width):
        at = slice(n * width, (n + 1) * width)
        out = dot(gated[...], w_o[:, at]).astype(BF16)
        part[:, :, at] = out.reshape(part.shape[0], part.shape[1], width)


def finish(inside, eff, s_in, gate, gain, w_o, parts):
    rows = inside.shape[0]
    vmem = pl.BlockSpec(memory_space=pltpu.VMEM)
    return pl.pallas_call(
        finish_kernel,
        in_specs=[vmem] * 6,
        out_specs=vmem,
        out_shape=jax.ShapeDtypeStruct((parts, rows // parts, w_o.shape[1]), BF16),
        scratch_shapes=[pltpu.VMEM(inside.shape, BF16)],
        compiler_params=pltpu.CompilerParams(vmem_limit_bytes=VMEM_LIMIT),
        name="gate_and_project",
    )(inside, eff, s_in, gate, gain.reshape(1, -1), w_o)


def scatter_kernel(part, out, relay, sums, land, rsend, rrecv, dsend, drecv):
    c = lax.axis_index("ctx")
    z = lax.axis_index("head")
    up, down, far = lax.rem(z + 1, 4), lax.rem(z + 3, 4), lax.rem(z + 2, 4)
    width = part.shape[2] // 2
    lo, hi = slice(0, width), slice(width, 2 * width)

    barrier = pltpu.get_barrier_semaphore()
    for peer in (up, down):
        pl.semaphore_signal(barrier, inc=1, device_id=(c, peer), device_id_type=MESH)
    pl.semaphore_wait(barrier, 2)

    relays = (
        remote(part.at[far, :, lo], relay.at[0], rsend.at[0], rrecv.at[0], c, up),
        remote(part.at[far, :, hi], relay.at[1], rsend.at[1], rrecv.at[1], c, down),
    )
    direct = (
        remote(part.at[up, :, hi], land.at[0, :, hi], dsend.at[0], drecv.at[0], c, up),
        remote(part.at[down, :, lo], land.at[1, :, lo], dsend.at[1], drecv.at[1], c, down),
    )
    summed = (
        remote(sums.at[0], land.at[0, :, lo], dsend.at[2], drecv.at[2], c, up),
        remote(sums.at[1], land.at[1, :, hi], dsend.at[3], drecv.at[3], c, down),
    )
    for copy in relays + direct:
        copy.start()
    for k, (peer, half) in enumerate(((up, lo), (down, hi))):
        relays[k].wait_recv()
        sums[k] = (part[peer, :, half].astype(F32) + relay[k].astype(F32)).astype(BF16)
        summed[k].start()
    for copy in direct + summed:
        copy.wait_recv()
    out[...] = (part[z].astype(F32) + land[0].astype(F32) + land[1].astype(F32)).astype(BF16)
    for copy in relays + direct + summed:
        copy.wait_send()


def scatter(part):
    parts, rows, width = part.shape
    vmem = pl.BlockSpec(memory_space=pltpu.VMEM)
    return pl.pallas_call(
        scatter_kernel,
        in_specs=[vmem],
        out_specs=vmem,
        out_shape=jax.ShapeDtypeStruct((rows, width), BF16),
        scratch_shapes=[
            pltpu.VMEM((2, rows, width // 2), BF16),
            pltpu.VMEM((2, rows, width // 2), BF16),
            pltpu.VMEM((2, rows, width), BF16),
            pltpu.SemaphoreType.DMA((2,)),
            pltpu.SemaphoreType.DMA((2,)),
            pltpu.SemaphoreType.DMA((4,)),
            pltpu.SemaphoreType.DMA((4,)),
        ],
        compiler_params=pltpu.CompilerParams(
            collective_id=1, has_side_effects=True, vmem_limit_bytes=VMEM_LIMIT
        ),
        name="sum_over_heads",
    )(part)


def local(
    activations, w_q, w_k, w_v, w_z, w_a, w_b, conv_q, conv_k, conv_v, a_log, dt_bias, norm_gain, w_o
):
    length = activations.shape[0]
    ctx = lax.axis_size("ctx")
    raw_q = jnp.dot(activations, w_q, preferred_element_type=F32).astype(BF16)
    raw_k = jnp.dot(activations, w_k, preferred_element_type=F32).astype(BF16)
    raw_v = jnp.dot(activations, w_v, preferred_element_type=F32).astype(BF16)
    tail = jnp.concatenate([raw[length - HALO :] for raw in (raw_q, raw_k, raw_v)], 1)
    halo = lax.ppermute(tail, "ctx", [(i, i + 1) for i in range(ctx - 1)])
    beta = jax.nn.sigmoid(jnp.dot(activations, w_b, preferred_element_type=F32))
    rate = jnp.exp(a_log) * jax.nn.softplus(
        jnp.dot(activations, w_a, preferred_element_type=F32) + dt_bias
    )
    cum = jnp.cumsum(-rate, 0)
    gate = jnp.dot(activations, w_z, preferred_element_type=F32)
    maps, inside, eff = gdn(raw_q, raw_k, raw_v, halo, conv_q, conv_k, conv_v, beta, cum, 2)
    states = exchange(maps, ctx // GROUP)
    part = finish(inside, eff, states, gate, norm_gain, w_o, lax.axis_size("head"))
    return scatter(part)


def solution(mesh):
    in_specs = (
        P("ctx", None),
        P(None, "head"),
        P(None, "head"),
        P(None, "head"),
        P(None, "head"),
        P(None, "head"),
        P(None, "head"),
        P(None, "head"),
        P(None, "head"),
        P(None, "head"),
        P("head"),
        P("head"),
        P(),
        P("head", None),
    )
    out_specs = P(("ctx", "head"), None)
    return jax.shard_map(local, mesh=mesh, in_specs=in_specs, out_specs=out_specs, check_vma=False)
```

```python
import functools
import math

import jax
import jax.numpy as jnp
from jax import lax
from jax.experimental import pallas as pl
from jax.experimental.pallas import tpu as pltpu
from jax.sharding import PartitionSpec as P

DK = 128
DV = 128
KERNEL = 4
HALO = 16
GROUP = 8
STEPS = 2
TILE = 256
MESH = pl.DeviceIdType.MESH
F32 = jnp.float32
BF16 = jnp.bfloat16
VMEM_LIMIT = 56 * 1024 * 1024
HIGHEST = lax.Precision.HIGHEST
NN = ((1,), (0,))
NT = ((1,), (1,))


def dot(a, b, dims=NN, precision=None):
    return lax.dot_general(a, b, (dims, ((), ())), preferred_element_type=F32, precision=precision)


def remote(src, dst, send, recv, ctx, head):
    return pltpu.make_async_remote_copy(
        src_ref=src, dst_ref=dst, send_sem=send, recv_sem=recv, device_id=(ctx, head), device_id_type=MESH
    )


def silu(x):
    return x / (1.0 + jnp.exp(-x))


def unit(feature, scale):
    norm = jnp.sum(feature * feature, -1, keepdims=True) + 1e-06
    return feature * (lax.rsqrt(norm) * scale)


def column(row):
    n = row.shape[1]
    same = lax.broadcasted_iota(jnp.int32, (n, n), 0) == lax.broadcasted_iota(jnp.int32, (n, n), 1)
    return jnp.sum(jnp.where(same, jnp.broadcast_to(row, (n, n)), 0.0), 1, keepdims=True)


def pair(both):
    n = both.shape[0]
    zero = jnp.zeros((n, n), both.dtype)
    return jnp.concatenate(
        [jnp.concatenate([both[:, :n], zero], 1), jnp.concatenate([zero, both[:, n:]], 1)], 0
    )


def invert(blocks):
    n = blocks[0].shape[0]
    row_at = lax.broadcasted_iota(jnp.int32, (n, 2 * n), 0)
    col_at = lax.broadcasted_iota(jnp.int32, (n, 2 * n), 1)
    differ = row_at ^ (col_at & (n - 1))
    one = jnp.where(differ == 0, 1.0, 0.0).astype(BF16)
    inverses = None
    width = 1
    while width < n:
        mask = jnp.where((differ >= width) & (differ < 2 * width), 1.0, 0.0).astype(BF16)
        lows = [block * mask for block in blocks]
        if inverses is None:
            inverses = [one - low for low in lows]
        else:
            right = [dot(low, pair(inv)).astype(BF16) for low, inv in zip(lows, inverses)]
            left = [dot(inv, pair(r)).astype(BF16) for inv, r in zip(inverses, right)]
            inverses = [inv - l for inv, l in zip(inverses, left)]
        width *= 2
    return inverses


def compose(later, earlier):
    return later + earlier + dot(later[:, :DK].astype(BF16), earlier.astype(BF16))


def kernel(
    groups, act, w_q, w_k, w_v, w_z, w_at, w_bt, cq, ck, cv, a_log, dt_bias, gain, w_o,
    out,
    ext, vq, vk, vv, vz, vo, pad, colt, rowt, inside, eff, gate, gated,
    maps, land, total, land2, pref, state, sbuf, s_in,
    part, relay, sums, reduced,
    lsem, hsend, hrecv, send1, recv1, send2, recv2, send3, recv3, rsend, rrecv, dsend, drecv,
):
    c = lax.axis_index("ctx")
    z = lax.axis_index("head")
    ctx = groups * GROUP
    g = c // GROUP
    me = lax.rem(c, GROUP)
    base = g * GROUP
    up, down, far = lax.rem(z + 1, 4), lax.rem(z + 3, 4), lax.rem(z + 2, 4)
    rows = act.shape[0]
    half = rows // 2
    heads = maps.shape[0]
    per = heads // STEPS
    kw, vw = w_q.shape[1] // STEPS, w_v.shape[1] // STEPS
    keys = w_q.shape[1]

    def fetch(step):
        ks, vs = pl.ds(step * kw, kw), pl.ds(step * vw, vw)
        return [
            pltpu.make_async_copy(w_q.at[:, ks], vq.at[:, ks], lsem.at[1 + 3 * step]),
            pltpu.make_async_copy(w_k.at[:, ks], vk.at[:, ks], lsem.at[2 + 3 * step]),
            pltpu.make_async_copy(w_v.at[:, vs], vv.at[:, vs], lsem.at[3 + 3 * step]),
        ]

    own = pltpu.make_async_copy(act, ext.at[pl.ds(HALO, rows)], lsem.at[0])
    last = 1 + 3 * STEPS
    tail_copies = [
        pltpu.make_async_copy(w_z, vz, lsem.at[last]),
        pltpu.make_async_copy(w_o, vo, lsem.at[last + 1]),
    ]
    own.start()
    for copy in fetch(0):
        copy.start()

    barrier = pltpu.get_barrier_semaphore()

    def greet(ctx_at, head_at):
        pl.semaphore_signal(barrier, inc=1, device_id=(ctx_at, head_at), device_id_type=MESH)

    for d in range(1, GROUP):
        greet(base + lax.rem(me + d, GROUP), z)
    for d in range(1, groups):
        greet(lax.rem(g + d, groups) * GROUP + me, z)
    greet(c, up)
    greet(c, down)

    @pl.when(me == 0)
    def _():
        greet(lax.rem(c + ctx - 1, ctx), z)

    pl.semaphore_wait(barrier, GROUP - 1 + groups - 1 + 2 + jnp.where(me == GROUP - 1, 1, 0))

    def halo(to):
        return remote(
            act.at[pl.ds(rows - HALO, HALO)], ext.at[pl.ds(0, HALO)], hsend, hrecv, to, z
        )

    @pl.when(c < ctx - 1)
    def _():
        halo(c + 1).start()

    @pl.when(c == 0)
    def _():
        ext[0:HALO] = jnp.zeros((HALO, ext.shape[1]), BF16)

    own.wait()
    tokens = ext[HALO:]
    beta = 1.0 / (1.0 + jnp.exp(-dot(w_bt[...], tokens, NT)))
    raw = dot(w_at[...], tokens, NT) + column(dt_bias[...])
    soft = jnp.maximum(raw, 0.0) + jnp.log1p(jnp.exp(-jnp.abs(raw)))
    logdecay = -jnp.exp(column(a_log[...])) * soft
    upto = (
        lax.broadcasted_iota(jnp.int32, (rows, rows), 0) <= lax.broadcasted_iota(jnp.int32, (rows, rows), 1)
    )
    cum = dot(logdecay, jnp.where(upto, 1.0, 0.0), NN, HIGHEST)
    rowt[...] = cum
    both = jnp.concatenate([cum, beta], 0)
    colt[...] = jnp.concatenate([both] * (128 // both.shape[0]), 0).T

    @pl.when(c > 0)
    def _():
        halo(c).wait_recv()

    row_at = lax.broadcasted_iota(jnp.int32, (half, half), 0)
    col_at = lax.broadcasted_iota(jnp.int32, (half, half), 1)
    lower = row_at >= col_at
    eye = jnp.where(
        lax.broadcasted_iota(jnp.int32, (DK, DK), 0) == lax.broadcasted_iota(jnp.int32, (DK, DK), 1), 1.0, 0.0
    )

    def project(weights, at, to):
        for n in range(0, at[1], TILE):
            out_n = dot(ext[...], weights[:, at[0] + n : at[0] + n + TILE])
            pad[:, to + n : to + n + TILE] = out_n.astype(BF16).astype(F32)

    def smooth(at, taps, taps_at):
        w = taps[:, taps_at : taps_at + DK]
        sum_ = w[KERNEL - 1 : KERNEL] * pad[HALO:, at : at + DK]
        for back in range(1, KERNEL):
            tap = w[KERNEL - 1 - back : KERNEL - back]
            sum_ = sum_ + tap * pad[HALO - back : HALO - back + rows, at : at + DK]
        return silu(sum_)

    for step in range(STEPS):
        for copy in fetch(step):
            copy.wait()
        for copy in fetch(step + 1) if step + 1 < STEPS else tail_copies:
            copy.start()
        project(vq, (step * kw, kw), step * kw)
        project(vk, (step * kw, kw), keys + step * kw)
        project(vv, (step * vw, vw), 2 * keys + step * vw)
        items = []
        for h in range(step * kw // DK, (step + 1) * kw // DK):
            query = unit(smooth(h * DK, cq, h * DK), 1.0 / math.sqrt(DK))
            key = unit(smooth(keys + h * DK, ck, h * DK), 1.0)
            kb = key.astype(BF16)
            gram = dot(jnp.concatenate([query.astype(BF16), kb], 0), kb, NT)
            qk, kk = gram[:rows], gram[rows:]
            key_t = key.T
            for j in range(2 * h, 2 * h + 2):
                value = smooth(2 * keys + j * DV, cv, j * DV)
                col = colt[:, j : j + 1]
                row = rowt[j : j + 1, :]
                b = colt[:, heads + j : heads + j + 1]
                f11 = jnp.exp(jnp.where(lower, col[:half] - row[:, :half], -1e30))
                f22 = jnp.exp(jnp.where(lower, col[half:] - row[:, half:], -1e30))
                f21 = jnp.exp(col[half:] - row[:, :half])
                a11 = (b[:half] * kk[:half, :half] * f11).astype(BF16)
                a22 = (b[half:] * kk[half:, half:] * f22).astype(BF16)
                a21 = (b[half:] * kk[half:, :half] * f21).astype(BF16)
                final = row[:, rows - 1 : rows]
                s1 = jnp.concatenate([qk[:half, :half] * f11, jnp.zeros((half, half), F32)], 1)
                s2 = jnp.concatenate([qk[half:, :half] * f21, qk[half:, half:] * f22], 1)
                left = jnp.concatenate([s1, s2, key_t * jnp.exp(final - row)], 0).astype(BF16)
                grow = jnp.exp(col)
                rhs = jnp.concatenate([key * (grow * b), value * b], 1).astype(BF16)
                items.append((j, jnp.concatenate([a11, a22], 1), a21, left, rhs, grow * query, final))
        inverses = invert([item[1] for item in items])
        for (j, _, a21, left, rhs, queries, final), inv in zip(items, inverses):
            x11, x22 = inv[:, :half], inv[:, half:]
            x21 = -dot(x22, dot(a21, x11).astype(BF16))
            whole = jnp.concatenate(
                [
                    jnp.concatenate([x11, jnp.zeros_like(x11)], 1),
                    jnp.concatenate([x21.astype(BF16), x22], 1),
                ],
                0,
            )
            wu = dot(whole, rhs).astype(BF16)
            res = dot(left, wu)
            at = slice(j * DV, (j + 1) * DV)
            inside[:, at] = res[:rows, DK:]
            eff[:, at] = (queries - res[:rows, :DK]).astype(BF16)
            first = (jnp.exp(final) - 1.0) * eye - res[rows:, :DK]
            maps[j] = jnp.concatenate([first, res[rows:, DK:]], 1).astype(BF16)
        for j in range(step * per, (step + 1) * per):

            @pl.when(j != me)
            def _(j=j):
                remote(maps.at[j], land.at[me], send1.at[j], recv1.at[me], base + j, z).start()

            @pl.when(j == me)
            def _(j=j):
                land[me] = maps[j]

    for copy in tail_copies:
        copy.wait()
    for n in range(0, gate.shape[1], TILE):
        raw_gate = dot(ext[HALO:], vz[:, n : n + TILE])
        gains = jnp.concatenate([gain[...]] * (TILE // DV), 1)
        gate[:, n : n + TILE] = silu(raw_gate) * gains

    for j in range(GROUP):

        @pl.when(j != me)
        def _(j=j):
            remote(maps.at[j], land.at[j], send1.at[j], recv1.at[j], base + j, z).wait_recv()

    m = [land[j].astype(F32) for j in range(GROUP)]
    p01, p23, p45, p67 = (compose(m[2 * k + 1], m[2 * k]) for k in range(4))
    p03, p47 = compose(p23, p01), compose(p67, p45)
    total[...] = compose(p47, p03).astype(BF16)
    for other in range(1, groups):

        @pl.when(g < other)
        def _(other=other):
            remote(total, land2.at[g], send2.at[other], recv2.at[g], other * GROUP + me, z).start()

    p05 = compose(p45, p03)
    for j, item in enumerate((m[0], p01, compose(m[2], p01), p03, compose(m[4], p03), p05, compose(m[6], p05))):
        pref[j] = item

    state[...] = jnp.zeros_like(state)
    for other in range(groups - 1):

        @pl.when(other < g)
        def _(other=other):
            remote(total, land2.at[other], send2.at[0], recv2.at[other], other * GROUP + me, z).wait_recv()
            now = state[...]
            step = land2[other]
            state[...] = now + step[:, DK:].astype(F32) + dot(step[:, :DK], now.astype(BF16))

    now = state[...]
    low = now.astype(BF16)
    for j in range(GROUP):
        if j == 0:
            sbuf[j] = low
        else:
            item = pref[j - 1]
            sbuf[j] = (now + item[:, DK:] + dot(item[:, :DK].astype(BF16), low)).astype(BF16)

        @pl.when(j != me)
        def _(j=j):
            remote(sbuf.at[j], s_in.at[me], send3.at[j], recv3.at[me], base + j, z).start()

    s_in[me] = sbuf[me]

    for j in range(heads):

        @pl.when(j != me)
        def _(j=j):
            remote(sbuf.at[j], s_in.at[j], send3.at[j], recv3.at[j], base + j, z).wait_recv()

        at = slice(j * DV, (j + 1) * DV)
        core = inside[:, at] + dot(eff[:, at], s_in[j])
        scale = lax.rsqrt(jnp.mean(core * core, -1, keepdims=True) + 1e-06)
        gated[:, at] = (core * scale * gate[:, at]).astype(BF16)

    width = part.shape[2] // 2
    lo, hi = slice(0, width), slice(width, 2 * width)
    relays = (
        remote(part.at[far, :, lo], relay.at[0], rsend.at[0], rrecv.at[0], c, up),
        remote(part.at[far, :, hi], relay.at[1], rsend.at[1], rrecv.at[1], c, down),
    )
    direct = (
        remote(part.at[down, :, lo], reduced.at[1, :, lo], dsend.at[0], drecv.at[0], c, down),
        remote(part.at[up, :, hi], reduced.at[0, :, hi], dsend.at[1], drecv.at[1], c, up),
    )
    summed = (
        remote(sums.at[0], reduced.at[0, :, lo], dsend.at[2], drecv.at[2], c, up),
        remote(sums.at[1], reduced.at[1, :, hi], dsend.at[3], drecv.at[3], c, down),
    )
    for k in range(2):
        for n in range(k * width, (k + 1) * width, TILE):
            tile = dot(gated[...], vo[:, n : n + TILE]).astype(BF16)
            part[:, :, n : n + TILE] = tile.reshape(part.shape[0], part.shape[1], TILE)
        relays[k].start()
        direct[k].start()
    for k, (peer, side) in enumerate(((up, lo), (down, hi))):
        relays[k].wait_recv()
        sums[k] = (part[peer, :, side].astype(F32) + relay[k].astype(F32)).astype(BF16)
        summed[k].start()
    for copy in direct + summed:
        copy.wait_recv()
    out[...] = (part[z].astype(F32) + reduced[0].astype(F32) + reduced[1].astype(F32)).astype(BF16)

    @pl.when(c < ctx - 1)
    def _():
        halo(c + 1).wait_send()

    for j in range(GROUP):

        @pl.when(j != me)
        def _(j=j):
            remote(maps.at[j], land.at[me], send1.at[j], recv1.at[me], base + j, z).wait_send()
            remote(sbuf.at[j], s_in.at[me], send3.at[j], recv3.at[me], base + j, z).wait_send()

    for other in range(1, groups):

        @pl.when(g < other)
        def _(other=other):
            remote(total, land2.at[g], send2.at[other], recv2.at[g], other * GROUP + me, z).wait_send()

    for copy in relays + direct + summed:
        copy.wait_send()


def local(
    activations, w_q, w_k, w_v, w_z, w_a, w_b, conv_q, conv_k, conv_v, a_log, dt_bias, norm_gain, w_o
):
    rows, depth = activations.shape
    heads = a_log.shape[0]
    groups = lax.axis_size("ctx") // GROUP
    parts = lax.axis_size("head")
    keys, values, wide = w_q.shape[1], w_v.shape[1], w_o.shape[1]
    hbm = pl.BlockSpec(memory_space=pl.ANY)
    vmem = pl.BlockSpec(memory_space=pltpu.VMEM)
    dma = pltpu.SemaphoreType.DMA
    piece = rows // parts
    return pl.pallas_call(
        functools.partial(kernel, groups),
        in_specs=[hbm] * 5 + [vmem] * 8 + [hbm],
        out_specs=vmem,
        out_shape=jax.ShapeDtypeStruct((piece, wide), BF16),
        scratch_shapes=[
            pltpu.VMEM((HALO + rows, depth), BF16),
            pltpu.VMEM(w_q.shape, BF16),
            pltpu.VMEM(w_k.shape, BF16),
            pltpu.VMEM(w_v.shape, BF16),
            pltpu.VMEM(w_z.shape, BF16),
            pltpu.VMEM(w_o.shape, BF16),
            pltpu.VMEM((HALO + rows, 2 * keys + values), F32),
            pltpu.VMEM((rows, 128), F32),
            pltpu.VMEM((heads, rows), F32),
            pltpu.VMEM((rows, values), F32),
            pltpu.VMEM((rows, heads * DK), BF16),
            pltpu.VMEM((rows, values), F32),
            pltpu.VMEM((rows, values), BF16),
            pltpu.VMEM((heads, DK, DK + DV), BF16),
            pltpu.VMEM((GROUP, DK, DK + DV), BF16),
            pltpu.VMEM((DK, DK + DV), BF16),
            pltpu.VMEM((groups, DK, DK + DV), BF16),
            pltpu.VMEM((GROUP, DK, DK + DV), F32),
            pltpu.VMEM((DK, DV), F32),
            pltpu.VMEM((GROUP, DK, DV), BF16),
            pltpu.VMEM((GROUP, DK, DV), BF16),
            pltpu.VMEM((parts, piece, wide), BF16),
            pltpu.VMEM((2, piece, wide // 2), BF16),
            pltpu.VMEM((2, piece, wide // 2), BF16),
            pltpu.VMEM((2, piece, wide), BF16),
            dma((3 + 3 * STEPS,)),
            dma,
            dma,
            dma((GROUP,)),
            dma((GROUP,)),
            dma((groups,)),
            dma((groups,)),
            dma((GROUP,)),
            dma((GROUP,)),
            dma((2,)),
            dma((2,)),
            dma((4,)),
            dma((4,)),
        ],
        compiler_params=pltpu.CompilerParams(
            collective_id=0, has_side_effects=True, vmem_limit_bytes=VMEM_LIMIT
        ),
        name="gated_delta_layer",
    )(
        activations, w_q, w_k, w_v, w_z, jnp.transpose(w_a), jnp.transpose(w_b), conv_q, conv_k, conv_v,
        a_log.reshape(1, -1), dt_bias.reshape(1, -1), norm_gain.reshape(1, -1), w_o,
    )


def solution(mesh):
    in_specs = (
        P("ctx", None),
        P(None, "head"),
        P(None, "head"),
        P(None, "head"),
        P(None, "head"),
        P(None, "head"),
        P(None, "head"),
        P(None, "head"),
        P(None, "head"),
        P(None, "head"),
        P("head"),
        P("head"),
        P(),
        P("head", None),
    )
    out_specs = P(("ctx", "head"), None)
    return jax.shard_map(local, mesh=mesh, in_specs=in_specs, out_specs=out_specs, check_vma=False)
```

```python
import functools
import math

import jax
import jax.numpy as jnp
from jax import lax
from jax.experimental import pallas as pl
from jax.experimental.pallas import tpu as pltpu
from jax.sharding import PartitionSpec as P

DK = 128
DV = 128
KERNEL = 4
HALO = 16
GROUP = 8
STEPS = 2
TILE = 256
MESH = pl.DeviceIdType.MESH
F32 = jnp.float32
BF16 = jnp.bfloat16
VMEM_LIMIT = 56 * 1024 * 1024
HIGHEST = lax.Precision.HIGHEST
NN = ((1,), (0,))
NT = ((1,), (1,))


def dot(a, b, dims=NN, precision=None):
    return lax.dot_general(a, b, (dims, ((), ())), preferred_element_type=F32, precision=precision)


def remote(src, dst, send, recv, ctx, head):
    return pltpu.make_async_remote_copy(
        src_ref=src, dst_ref=dst, send_sem=send, recv_sem=recv, device_id=(ctx, head), device_id_type=MESH
    )


def silu(x):
    return x / (1.0 + jnp.exp(-x))


def unit(feature, scale):
    norm = jnp.sum(feature * feature, -1, keepdims=True) + 1e-06
    return feature * (lax.rsqrt(norm) * scale)


def column(row):
    n = row.shape[1]
    same = lax.broadcasted_iota(jnp.int32, (n, n), 0) == lax.broadcasted_iota(jnp.int32, (n, n), 1)
    return jnp.sum(jnp.where(same, jnp.broadcast_to(row, (n, n)), 0.0), 1, keepdims=True)


def pair(both):
    n = both.shape[0]
    zero = jnp.zeros((n, n), both.dtype)
    return jnp.concatenate(
        [jnp.concatenate([both[:, :n], zero], 1), jnp.concatenate([zero, both[:, n:]], 1)], 0
    )


def invert(blocks, found):
    n = blocks[0].shape[0]
    row_at = lax.broadcasted_iota(jnp.int32, (n, 2 * n), 0)
    col_at = lax.broadcasted_iota(jnp.int32, (n, 2 * n), 1)
    differ = row_at ^ (col_at & (n - 1))
    one = jnp.where(differ == 0, 1.0, 0.0).astype(BF16)
    inverses = None
    width = 1
    while width < n:
        mask = jnp.where((differ >= width) & (differ < 2 * width), 1.0, 0.0).astype(BF16)
        lows = [block * mask for block in blocks]
        if inverses is None:
            inverses = [one - low for low in lows]
        else:
            right = [dot(low, pair(inv)).astype(BF16) for low, inv in zip(lows, inverses)]
            yield
            left = [dot(inv, pair(r)).astype(BF16) for inv, r in zip(inverses, right)]
            inverses = [inv - l for inv, l in zip(inverses, left)]
            yield
        width *= 2
    found.extend(inverses)


def compose(later, earlier):
    return later + earlier + dot(later[:, :DK].astype(BF16), earlier.astype(BF16))


def kernel(
    groups, act, w_q, w_k, w_v, w_z, w_at, w_bt, cq, ck, cv, a_log, dt_bias, gain, w_o,
    out,
    ext, vq, vk, vv, vz, vo, pad, colt, rowt, inside, eff, gate, gated,
    maps, land, total, land2, pref, state, sbuf, s_in,
    part, relay, sums, reduced,
    lsem, hsend, hrecv, send1, recv1, send2, recv2, send3, recv3, rsend, rrecv, dsend, drecv,
):
    c = lax.axis_index("ctx")
    z = lax.axis_index("head")
    ctx = groups * GROUP
    g = c // GROUP
    me = lax.rem(c, GROUP)
    base = g * GROUP
    up, down, far = lax.rem(z + 1, 4), lax.rem(z + 3, 4), lax.rem(z + 2, 4)
    rows = act.shape[0]
    half = rows // 2
    heads = maps.shape[0]
    per = heads // STEPS
    kw, vw = w_q.shape[1] // STEPS, w_v.shape[1] // STEPS
    keys = w_q.shape[1]

    def fetch(step):
        ks, vs = pl.ds(step * kw, kw), pl.ds(step * vw, vw)
        return [
            pltpu.make_async_copy(w_q.at[:, ks], vq.at[:, ks], lsem.at[1 + 3 * step]),
            pltpu.make_async_copy(w_k.at[:, ks], vk.at[:, ks], lsem.at[2 + 3 * step]),
            pltpu.make_async_copy(w_v.at[:, vs], vv.at[:, vs], lsem.at[3 + 3 * step]),
        ]

    own = pltpu.make_async_copy(act, ext.at[pl.ds(HALO, rows)], lsem.at[0])
    last = 1 + 3 * STEPS
    tail_copies = [
        pltpu.make_async_copy(w_z, vz, lsem.at[last]),
        pltpu.make_async_copy(w_o, vo, lsem.at[last + 1]),
    ]
    own.start()
    for copy in fetch(0) + fetch(1):
        copy.start()

    barrier = pltpu.get_barrier_semaphore()

    def greet(ctx_at, head_at):
        pl.semaphore_signal(barrier, inc=1, device_id=(ctx_at, head_at), device_id_type=MESH)

    for d in range(1, GROUP):
        greet(base + lax.rem(me + d, GROUP), z)
    for d in range(1, groups):
        greet(lax.rem(g + d, groups) * GROUP + me, z)
    greet(c, up)
    greet(c, down)

    @pl.when(me == 0)
    def _():
        greet(lax.rem(c + ctx - 1, ctx), z)

    pl.semaphore_wait(barrier, GROUP - 1 + groups - 1 + 2 + jnp.where(me == GROUP - 1, 1, 0))

    def halo(to):
        return remote(
            act.at[pl.ds(rows - HALO, HALO)], ext.at[pl.ds(0, HALO)], hsend, hrecv, to, z
        )

    @pl.when(c < ctx - 1)
    def _():
        halo(c + 1).start()

    @pl.when(c == 0)
    def _():
        ext[0:HALO] = jnp.zeros((HALO, ext.shape[1]), BF16)

    def project(weights, n, to, first, count):
        out_n = dot(ext[first : first + count], weights[:, n : n + TILE])
        pad[first : first + count, to + n : to + n + TILE] = out_n.astype(BF16).astype(F32)

    def projections(step, first, count):
        todo = []
        for weights, width, to in ((vq, kw, 0), (vk, kw, keys), (vv, vw, 2 * keys)):
            for n in range(step * width, (step + 1) * width, TILE):
                todo.append(functools.partial(project, weights, n, to, first, count))
        return todo

    own.wait()
    tokens = ext[HALO:]
    beta = 1.0 / (1.0 + jnp.exp(-dot(w_bt[...], tokens, NT)))
    raw = dot(w_at[...], tokens, NT) + column(dt_bias[...])
    soft = jnp.maximum(raw, 0.0) + jnp.log1p(jnp.exp(-jnp.abs(raw)))
    logdecay = -jnp.exp(column(a_log[...])) * soft
    upto = (
        lax.broadcasted_iota(jnp.int32, (rows, rows), 0) <= lax.broadcasted_iota(jnp.int32, (rows, rows), 1)
    )
    cum = dot(logdecay, jnp.where(upto, 1.0, 0.0), NN, HIGHEST)
    rowt[...] = cum
    both = jnp.concatenate([cum, beta], 0)
    colt[...] = jnp.concatenate([both] * (128 // both.shape[0]), 0).T
    for copy in fetch(0):
        copy.wait()
    for copy in tail_copies:
        copy.start()
    for work in projections(0, HALO, rows):
        work()

    @pl.when(c > 0)
    def _():
        halo(c).wait_recv()

    for work in projections(0, 0, HALO):
        work()

    row_at = lax.broadcasted_iota(jnp.int32, (half, half), 0)
    col_at = lax.broadcasted_iota(jnp.int32, (half, half), 1)
    lower = row_at >= col_at
    eye = jnp.where(
        lax.broadcasted_iota(jnp.int32, (DK, DK), 0) == lax.broadcasted_iota(jnp.int32, (DK, DK), 1), 1.0, 0.0
    )

    def smooth(at, taps, taps_at):
        w = taps[:, taps_at : taps_at + DK]
        sum_ = w[KERNEL - 1 : KERNEL] * pad[HALO:, at : at + DK]
        for back in range(1, KERNEL):
            tap = w[KERNEL - 1 - back : KERNEL - back]
            sum_ = sum_ + tap * pad[HALO - back : HALO - back + rows, at : at + DK]
        return silu(sum_)

    def prepare(h, items):
        query = unit(smooth(h * DK, cq, h * DK), 1.0 / math.sqrt(DK))
        key = unit(smooth(keys + h * DK, ck, h * DK), 1.0)
        kb = key.astype(BF16)
        gram = dot(jnp.concatenate([query.astype(BF16), kb], 0), kb, NT)
        qk, kk = gram[:rows], gram[rows:]
        key_t = key.T
        for j in range(2 * h, 2 * h + 2):
            value = smooth(2 * keys + j * DV, cv, j * DV)
            col = colt[:, j : j + 1]
            row = rowt[j : j + 1, :]
            b = colt[:, heads + j : heads + j + 1]
            f11 = jnp.exp(jnp.where(lower, col[:half] - row[:, :half], -1e30))
            f22 = jnp.exp(jnp.where(lower, col[half:] - row[:, half:], -1e30))
            f21 = jnp.exp(col[half:] - row[:, :half])
            a11 = (b[:half] * kk[:half, :half] * f11).astype(BF16)
            a22 = (b[half:] * kk[half:, half:] * f22).astype(BF16)
            a21 = (b[half:] * kk[half:, :half] * f21).astype(BF16)
            final = row[:, rows - 1 : rows]
            s1 = jnp.concatenate([qk[:half, :half] * f11, jnp.zeros((half, half), F32)], 1)
            s2 = jnp.concatenate([qk[half:, :half] * f21, qk[half:, half:] * f22], 1)
            left = jnp.concatenate([s1, s2, key_t * jnp.exp(final - row)], 0).astype(BF16)
            grow = jnp.exp(col)
            rhs = jnp.concatenate([key * (grow * b), value * b], 1).astype(BF16)
            items.append((j, jnp.concatenate([a11, a22], 1), a21, left, rhs, grow * query, final))

    def conclude(items, inverses):
        halves = [(inv[:, :half], inv[:, half:]) for inv in inverses]
        lows = [dot(item[2], x11).astype(BF16) for item, (x11, _) in zip(items, halves)]
        yield
        corners = [-dot(x22, low) for low, (_, x22) in zip(lows, halves)]
        wholes = [
            jnp.concatenate(
                [
                    jnp.concatenate([x11, jnp.zeros_like(x11)], 1),
                    jnp.concatenate([x21.astype(BF16), x22], 1),
                ],
                0,
            )
            for x21, (x11, x22) in zip(corners, halves)
        ]
        yield
        solved = [dot(whole, item[4]).astype(BF16) for item, whole in zip(items, wholes)]
        yield
        results = [dot(item[3], wu) for item, wu in zip(items, solved)]
        for (j, _, _, _, _, queries, final), res in zip(items, results):
            first = (jnp.exp(final) - 1.0) * eye - res[rows:, :DK]
            maps[j] = jnp.concatenate([first, res[rows:, DK:]], 1).astype(BF16)
            at = slice(j * DV, (j + 1) * DV)
            inside[:, at] = res[:rows, DK:]
            eff[:, at] = (queries - res[:rows, :DK]).astype(BF16)
        yield

    def dispatch(step):
        for j in range(step * per, (step + 1) * per):

            @pl.when(j != me)
            def _(j=j):
                remote(maps.at[j], land.at[me], send1.at[j], recv1.at[me], base + j, z).start()

            @pl.when(j == me)
            def _(j=j):
                land[me] = maps[j]

    key_heads = kw // DK
    early, later = [], []
    for h in range(key_heads):
        prepare(h, early)
    for copy in fetch(1):
        copy.wait()
    for work in projections(1, 0, HALO + rows):
        work()
    for h in range(key_heads, 2 * key_heads):
        prepare(h, later)
    found = []
    for _ in invert([item[1] for item in early + later], found):
        pass
    for _ in conclude(early, found[:per]):
        pass
    dispatch(0)
    for _ in conclude(later, found[per:]):
        pass
    dispatch(1)

    for copy in tail_copies:
        copy.wait()
    for n in range(0, gate.shape[1], TILE):
        raw_gate = dot(ext[HALO:], vz[:, n : n + TILE])
        gains = jnp.concatenate([gain[...]] * (TILE // DV), 1)
        gate[:, n : n + TILE] = silu(raw_gate) * gains

    for j in range(GROUP):

        @pl.when(j != me)
        def _(j=j):
            remote(maps.at[j], land.at[j], send1.at[j], recv1.at[j], base + j, z).wait_recv()

    m = [land[j].astype(F32) for j in range(GROUP)]
    p01, p23, p45, p67 = (compose(m[2 * k + 1], m[2 * k]) for k in range(4))
    p03, p47 = compose(p23, p01), compose(p67, p45)
    total[...] = compose(p47, p03).astype(BF16)

    def first_total(other):
        return remote(
            total.at[:, pl.ds(DK, DV)], land2.at[0, :, pl.ds(DK, DV)], send2.at[other], recv2.at[0],
            other * GROUP + me, z,
        )

    for other in range(1, groups):

        @pl.when((g > 0) & (g < other))
        def _(other=other):
            remote(total, land2.at[g], send2.at[other], recv2.at[g], other * GROUP + me, z).start()

        @pl.when(g == 0)
        def _(other=other):
            first_total(other).start()

    p05 = compose(p45, p03)
    pref[0] = jnp.zeros((DK, DK + DV), F32)
    for j, item in enumerate((m[0], p01, compose(m[2], p01), p03, compose(m[4], p03), p05, compose(m[6], p05))):
        pref[j + 1] = item

    state[...] = jnp.zeros_like(state)

    @pl.when(g > 0)
    def _():
        first_total(0).wait_recv()
        state[...] = land2[0, :, DK:].astype(F32)

    for other in range(1, groups - 1):

        @pl.when(other < g)
        def _(other=other):
            remote(total, land2.at[other], send2.at[0], recv2.at[other], other * GROUP + me, z).wait_recv()
            now = state[...]
            step = land2[other]
            state[...] = now + step[:, DK:].astype(F32) + dot(step[:, :DK], now.astype(BF16))

    now = state[...]
    low = now.astype(BF16)

    def enter(j):
        item = pref[j]
        sbuf[j] = (now + item[:, DK:] + dot(item[:, :DK].astype(BF16), low)).astype(BF16)

    def entered(peer):
        return remote(sbuf.at[peer], s_in.at[me], send3.at[peer], recv3.at[me], base + peer, z)

    for batch in ((4, 5, 3, 6), (2, 7, 1, 0)):
        peers = [lax.rem(me + d, GROUP) for d in batch]
        for peer in peers:
            enter(peer)
        for d, peer in zip(batch, peers):
            if d:
                entered(peer).start()
    s_in[me] = sbuf[me]

    for batch in ((0, 1, 7), (2, 6), (3, 5, 4)):
        members = [lax.rem(me + d, GROUP) for d in batch]
        for d, j in zip(batch, members):
            if d:
                remote(sbuf.at[j], s_in.at[j], send3.at[j], recv3.at[j], base + j, z).wait_recv()
        cores = []
        for j in members:
            at = pl.ds(pl.multiple_of(j * DV, DV), DV)
            cores.append((at, inside[:, at] + dot(eff[:, at], s_in[j])))
        for at, core in cores:
            scale = lax.rsqrt(jnp.mean(core * core, -1, keepdims=True) + 1e-06)
            gated[:, at] = (core * scale * gate[:, at]).astype(BF16)

    width = part.shape[2] // 2
    lo, hi = slice(0, width), slice(width, 2 * width)
    relays = (
        remote(part.at[far, :, lo], relay.at[0], rsend.at[0], rrecv.at[0], c, up),
        remote(part.at[far, :, hi], relay.at[1], rsend.at[1], rrecv.at[1], c, down),
    )
    direct = (
        remote(part.at[down, :, lo], reduced.at[1, :, lo], dsend.at[0], drecv.at[0], c, down),
        remote(part.at[up, :, hi], reduced.at[0, :, hi], dsend.at[1], drecv.at[1], c, up),
    )
    summed = (
        remote(sums.at[0], reduced.at[0, :, lo], dsend.at[2], drecv.at[2], c, up),
        remote(sums.at[1], reduced.at[1, :, hi], dsend.at[3], drecv.at[3], c, down),
    )
    for k in range(2):
        for n in range(k * width, (k + 1) * width, TILE):
            tile = dot(gated[...], vo[:, n : n + TILE]).astype(BF16)
            part[:, :, n : n + TILE] = tile.reshape(part.shape[0], part.shape[1], TILE)
        relays[k].start()
        direct[k].start()
    for k, (peer, side) in enumerate(((up, lo), (down, hi))):
        relays[k].wait_recv()
        sums[k] = (part[peer, :, side].astype(F32) + relay[k].astype(F32)).astype(BF16)
        summed[k].start()
    for copy in direct + summed:
        copy.wait_recv()
    out[...] = (part[z].astype(F32) + reduced[0].astype(F32) + reduced[1].astype(F32)).astype(BF16)

    @pl.when(c < ctx - 1)
    def _():
        halo(c + 1).wait_send()

    for j in range(GROUP):

        @pl.when(j != me)
        def _(j=j):
            remote(maps.at[j], land.at[me], send1.at[j], recv1.at[me], base + j, z).wait_send()
            remote(sbuf.at[j], s_in.at[me], send3.at[j], recv3.at[me], base + j, z).wait_send()

    for other in range(1, groups):

        @pl.when((g > 0) & (g < other))
        def _(other=other):
            remote(total, land2.at[g], send2.at[other], recv2.at[g], other * GROUP + me, z).wait_send()

        @pl.when(g == 0)
        def _(other=other):
            first_total(other).wait_send()

    for copy in relays + direct + summed:
        copy.wait_send()


def local(
    activations, w_q, w_k, w_v, w_z, w_a, w_b, conv_q, conv_k, conv_v, a_log, dt_bias, norm_gain, w_o
):
    rows, depth = activations.shape
    heads = a_log.shape[0]
    groups = lax.axis_size("ctx") // GROUP
    parts = lax.axis_size("head")
    keys, values, wide = w_q.shape[1], w_v.shape[1], w_o.shape[1]
    hbm = pl.BlockSpec(memory_space=pl.ANY)
    vmem = pl.BlockSpec(memory_space=pltpu.VMEM)
    dma = pltpu.SemaphoreType.DMA
    piece = rows // parts
    return pl.pallas_call(
        functools.partial(kernel, groups),
        in_specs=[hbm] * 5 + [vmem] * 8 + [hbm],
        out_specs=vmem,
        out_shape=pltpu.VMEM((piece, wide), BF16),
        scratch_shapes=[
            pltpu.VMEM((HALO + rows, depth), BF16),
            pltpu.VMEM(w_q.shape, BF16),
            pltpu.VMEM(w_k.shape, BF16),
            pltpu.VMEM(w_v.shape, BF16),
            pltpu.VMEM(w_z.shape, BF16),
            pltpu.VMEM(w_o.shape, BF16),
            pltpu.VMEM((HALO + rows, 2 * keys + values), F32),
            pltpu.VMEM((rows, 128), F32),
            pltpu.VMEM((heads, rows), F32),
            pltpu.VMEM((rows, values), F32),
            pltpu.VMEM((rows, heads * DK), BF16),
            pltpu.VMEM((rows, values), F32),
            pltpu.VMEM((rows, values), BF16),
            pltpu.VMEM((heads, DK, DK + DV), BF16),
            pltpu.VMEM((GROUP, DK, DK + DV), BF16),
            pltpu.VMEM((DK, DK + DV), BF16),
            pltpu.VMEM((groups, DK, DK + DV), BF16),
            pltpu.VMEM((GROUP, DK, DK + DV), F32),
            pltpu.VMEM((DK, DV), F32),
            pltpu.VMEM((GROUP, DK, DV), BF16),
            pltpu.VMEM((GROUP, DK, DV), BF16),
            pltpu.VMEM((parts, piece, wide), BF16),
            pltpu.VMEM((2, piece, wide // 2), BF16),
            pltpu.VMEM((2, piece, wide // 2), BF16),
            pltpu.VMEM((2, piece, wide), BF16),
            dma((3 + 3 * STEPS,)),
            dma,
            dma,
            dma((GROUP,)),
            dma((GROUP,)),
            dma((groups,)),
            dma((groups,)),
            dma((GROUP,)),
            dma((GROUP,)),
            dma((2,)),
            dma((2,)),
            dma((4,)),
            dma((4,)),
        ],
        compiler_params=pltpu.CompilerParams(
            collective_id=0, has_side_effects=True, vmem_limit_bytes=VMEM_LIMIT
        ),
        name="gated_delta_layer",
    )(
        activations, w_q, w_k, w_v, w_z, jnp.transpose(w_a), jnp.transpose(w_b), conv_q, conv_k, conv_v,
        a_log.reshape(1, -1), dt_bias.reshape(1, -1), norm_gain.reshape(1, -1), w_o,
    )


def solution(mesh):
    in_specs = (
        P("ctx", None),
        P(None, "head"),
        P(None, "head"),
        P(None, "head"),
        P(None, "head"),
        P(None, "head"),
        P(None, "head"),
        P(None, "head"),
        P(None, "head"),
        P(None, "head"),
        P("head"),
        P("head"),
        P(),
        P("head", None),
    )
    out_specs = P(("ctx", "head"), None)
    return jax.shard_map(local, mesh=mesh, in_specs=in_specs, out_specs=out_specs, check_vma=False)
```

```python
import functools
import math

import jax
import jax.numpy as jnp
from jax import lax
from jax.experimental import pallas as pl
from jax.experimental.pallas import tpu as pltpu
from jax.sharding import PartitionSpec as P

DK = 128
DV = 128
KERNEL = 4
HALO = 16
GROUP = 8
STEPS = 2
TILE = 256
MESH = pl.DeviceIdType.MESH
F32 = jnp.float32
BF16 = jnp.bfloat16
VMEM_LIMIT = 56 * 1024 * 1024
HIGHEST = lax.Precision.HIGHEST
NN = ((1,), (0,))
NT = ((1,), (1,))


def dot(a, b, dims=NN, precision=None):
    return lax.dot_general(a, b, (dims, ((), ())), preferred_element_type=F32, precision=precision)


def remote(src, dst, send, recv, ctx, head):
    return pltpu.make_async_remote_copy(
        src_ref=src, dst_ref=dst, send_sem=send, recv_sem=recv, device_id=(ctx, head), device_id_type=MESH
    )


def silu(x):
    return x / (1.0 + jnp.exp(-x))


def unit(feature, scale):
    norm = jnp.sum(feature * feature, -1, keepdims=True) + 1e-06
    return feature * (lax.rsqrt(norm) * scale)


def column(row):
    n = row.shape[1]
    same = lax.broadcasted_iota(jnp.int32, (n, n), 0) == lax.broadcasted_iota(jnp.int32, (n, n), 1)
    return jnp.sum(jnp.where(same, jnp.broadcast_to(row, (n, n)), 0.0), 1, keepdims=True)


def pair(both):
    n = both.shape[0]
    zero = jnp.zeros((n, n), both.dtype)
    return jnp.concatenate(
        [jnp.concatenate([both[:, :n], zero], 1), jnp.concatenate([zero, both[:, n:]], 1)], 0
    )


def invert(blocks, found):
    n = blocks[0].shape[0]
    row_at = lax.broadcasted_iota(jnp.int32, (n, 2 * n), 0)
    col_at = lax.broadcasted_iota(jnp.int32, (n, 2 * n), 1)
    differ = row_at ^ (col_at & (n - 1))
    one = jnp.where(differ == 0, 1.0, 0.0).astype(BF16)
    inverses = None
    width = 1
    while width < n:
        mask = jnp.where((differ >= width) & (differ < 2 * width), 1.0, 0.0).astype(BF16)
        lows = [block * mask for block in blocks]
        if inverses is None:
            inverses = [one - low for low in lows]
        else:
            right = [dot(low, pair(inv)).astype(BF16) for low, inv in zip(lows, inverses)]
            yield
            left = [dot(inv, pair(r)).astype(BF16) for inv, r in zip(inverses, right)]
            inverses = [inv - l for inv, l in zip(inverses, left)]
            yield
        width *= 2
    found.extend(inverses)


def compose(later, earlier):
    return later + earlier + dot(later[:, :DK].astype(BF16), earlier.astype(BF16))


def kernel(
    groups, act, w_q, w_k, w_v, w_z, w_at, w_bt, cq, ck, cv, a_log, dt_bias, gain, w_o,
    out,
    ext, vq, vk, vv, vz, vo, pad, colt, rowt, keyb, solutions, inside, eff, gate, gated,
    maps, land, total, land2, pref, state, sbuf, s_in,
    part, relay, sums, reduced,
    lsem, hsend, hrecv, send1, recv1, send2, recv2, send3, recv3, rsend, rrecv, dsend, drecv,
):
    c = lax.axis_index("ctx")
    z = lax.axis_index("head")
    ctx = groups * GROUP
    g = c // GROUP
    me = lax.rem(c, GROUP)
    base = g * GROUP
    up, down, far = lax.rem(z + 1, 4), lax.rem(z + 3, 4), lax.rem(z + 2, 4)
    rows = act.shape[0]
    half = rows // 2
    heads = maps.shape[0]
    per = heads // STEPS
    kw, vw = w_q.shape[1] // STEPS, w_v.shape[1] // STEPS
    keys = w_q.shape[1]

    def fetch(step):
        ks, vs = pl.ds(step * kw, kw), pl.ds(step * vw, vw)
        return [
            pltpu.make_async_copy(w_k.at[:, ks], vk.at[:, ks], lsem.at[1 + 2 * step]),
            pltpu.make_async_copy(w_v.at[:, vs], vv.at[:, vs], lsem.at[2 + 2 * step]),
        ]

    own = pltpu.make_async_copy(act, ext.at[pl.ds(HALO, rows)], lsem.at[0])
    last = 1 + 2 * STEPS
    tail_copies = [
        pltpu.make_async_copy(w_q, vq, lsem.at[last]),
        pltpu.make_async_copy(w_z, vz, lsem.at[last + 1]),
        pltpu.make_async_copy(w_o, vo, lsem.at[last + 2]),
    ]
    own.start()
    for copy in fetch(0) + fetch(1):
        copy.start()

    barrier = pltpu.get_barrier_semaphore()

    def greet(ctx_at, head_at):
        pl.semaphore_signal(barrier, inc=1, device_id=(ctx_at, head_at), device_id_type=MESH)

    for d in range(1, GROUP):
        greet(base + lax.rem(me + d, GROUP), z)
    for d in range(1, groups):
        greet(lax.rem(g + d, groups) * GROUP + me, z)
    greet(c, up)
    greet(c, down)

    @pl.when(me == 0)
    def _():
        greet(lax.rem(c + ctx - 1, ctx), z)

    pl.semaphore_wait(barrier, GROUP - 1 + groups - 1 + 2 + jnp.where(me == GROUP - 1, 1, 0))

    def halo(to):
        return remote(
            act.at[pl.ds(rows - HALO, HALO)], ext.at[pl.ds(0, HALO)], hsend, hrecv, to, z
        )

    @pl.when(c < ctx - 1)
    def _():
        halo(c + 1).start()

    @pl.when(c == 0)
    def _():
        ext[0:HALO] = jnp.zeros((HALO, ext.shape[1]), BF16)

    def project(weights, n, to, first, count):
        out_n = dot(ext[first : first + count], weights[:, n : n + TILE])
        pad[first : first + count, to + n : to + n + TILE] = out_n.astype(BF16).astype(F32)

    def projections(step, first, count):
        todo = []
        for weights, width, to in ((vk, kw, keys), (vv, vw, 2 * keys)):
            for n in range(step * width, (step + 1) * width, TILE):
                todo.append(functools.partial(project, weights, n, to, first, count))
        return todo

    own.wait()
    tokens = ext[HALO:]
    beta = 1.0 / (1.0 + jnp.exp(-dot(w_bt[...], tokens, NT)))
    raw = dot(w_at[...], tokens, NT) + column(dt_bias[...])
    soft = jnp.maximum(raw, 0.0) + jnp.log1p(jnp.exp(-jnp.abs(raw)))
    logdecay = -jnp.exp(column(a_log[...])) * soft
    upto = (
        lax.broadcasted_iota(jnp.int32, (rows, rows), 0) <= lax.broadcasted_iota(jnp.int32, (rows, rows), 1)
    )
    cum = dot(logdecay, jnp.where(upto, 1.0, 0.0), NN, HIGHEST)
    rowt[...] = cum
    both = jnp.concatenate([cum, beta], 0)
    colt[...] = jnp.concatenate([both] * (128 // both.shape[0]), 0).T
    for copy in fetch(0):
        copy.wait()
    for copy in tail_copies:
        copy.start()
    for work in projections(0, HALO, rows):
        work()

    @pl.when(c > 0)
    def _():
        halo(c).wait_recv()

    for work in projections(0, 0, HALO):
        work()

    row_at = lax.broadcasted_iota(jnp.int32, (half, half), 0)
    col_at = lax.broadcasted_iota(jnp.int32, (half, half), 1)
    lower = row_at >= col_at
    eye = jnp.where(
        lax.broadcasted_iota(jnp.int32, (DK, DK), 0) == lax.broadcasted_iota(jnp.int32, (DK, DK), 1), 1.0, 0.0
    )

    def smooth(at, taps, taps_at):
        w = taps[:, taps_at : taps_at + DK]
        sum_ = w[KERNEL - 1 : KERNEL] * pad[HALO:, at : at + DK]
        for back in range(1, KERNEL):
            tap = w[KERNEL - 1 - back : KERNEL - back]
            sum_ = sum_ + tap * pad[HALO - back : HALO - back + rows, at : at + DK]
        return silu(sum_)

    def factors(j):
        col, row = colt[:, j : j + 1], rowt[j : j + 1, :]
        f11 = jnp.exp(jnp.where(lower, col[:half] - row[:, :half], -1e30))
        f22 = jnp.exp(jnp.where(lower, col[half:] - row[:, half:], -1e30))
        f21 = jnp.exp(col[half:] - row[:, :half])
        return f11, f22, f21

    def prepare(h, items):
        key = unit(smooth(keys + h * DK, ck, h * DK), 1.0)
        kb = key.astype(BF16)
        keyb[:, h * DK : (h + 1) * DK] = kb
        kk = dot(kb, kb, NT)
        key_t = key.T
        for j in range(2 * h, 2 * h + 2):
            value = smooth(2 * keys + j * DV, cv, j * DV)
            f11, f22, f21 = factors(j)
            b = colt[:, heads + j : heads + j + 1]
            row = rowt[j : j + 1, :]
            a11 = (b[:half] * kk[:half, :half] * f11).astype(BF16)
            a22 = (b[half:] * kk[half:, half:] * f22).astype(BF16)
            a21 = (b[half:] * kk[half:, :half] * f21).astype(BF16)
            final = row[:, rows - 1 : rows]
            carried = (key_t * jnp.exp(final - row)).astype(BF16)
            rhs = jnp.concatenate([key * (jnp.exp(colt[:, j : j + 1]) * b), value * b], 1).astype(BF16)
            items.append((j, jnp.concatenate([a11, a22], 1), a21, carried, rhs, final))

    def conclude(items, inverses):
        halves = [(inv[:, :half], inv[:, half:]) for inv in inverses]
        lows = [dot(item[2], x11).astype(BF16) for item, (x11, _) in zip(items, halves)]
        yield
        corners = [-dot(x22, low) for low, (_, x22) in zip(lows, halves)]
        wholes = [
            jnp.concatenate(
                [
                    jnp.concatenate([x11, jnp.zeros_like(x11)], 1),
                    jnp.concatenate([x21.astype(BF16), x22], 1),
                ],
                0,
            )
            for x21, (x11, x22) in zip(corners, halves)
        ]
        yield
        solved = [dot(whole, item[4]).astype(BF16) for item, whole in zip(items, wholes)]
        yield
        results = [dot(item[3], wu) for item, wu in zip(items, solved)]
        for (j, _, _, _, _, final), res, wu in zip(items, results, solved):
            first = (jnp.exp(final) - 1.0) * eye - res[:, :DK]
            maps[j] = jnp.concatenate([first, res[:, DK:]], 1).astype(BF16)
            solutions[j] = wu
        yield

    def dispatch(step):
        for j in range(step * per, (step + 1) * per):

            @pl.when(j != me)
            def _(j=j):
                remote(maps.at[j], land.at[me], send1.at[j], recv1.at[me], base + j, z).start()

            @pl.when(j == me)
            def _(j=j):
                land[me] = maps[j]

    key_heads = kw // DK
    early, later = [], []
    for h in range(key_heads):
        prepare(h, early)
    for copy in fetch(1):
        copy.wait()
    for work in projections(1, 0, HALO + rows):
        work()
    for h in range(key_heads, 2 * key_heads):
        prepare(h, later)
    found = []
    for _ in invert([item[1] for item in early + later], found):
        pass
    for _ in conclude(early, found[:per]):
        pass
    dispatch(0)
    for _ in conclude(later, found[per:]):
        pass
    dispatch(1)

    tail_copies[0].wait()
    for n in range(0, keys, TILE):
        project(vq, n, 0, 0, HALO + rows)
    scores = []
    for h in range(keys // DK):
        query = unit(smooth(h * DK, cq, h * DK), 1.0 / math.sqrt(DK))
        qk = dot(query.astype(BF16), keyb[:, h * DK : (h + 1) * DK], NT)
        for j in range(2 * h, 2 * h + 2):
            f11, f22, f21 = factors(j)
            s1 = jnp.concatenate([qk[:half, :half] * f11, jnp.zeros((half, half), F32)], 1)
            s2 = jnp.concatenate([qk[half:, :half] * f21, qk[half:, half:] * f22], 1)
            both = jnp.concatenate([s1, s2], 0).astype(BF16)
            scores.append((both, jnp.exp(colt[:, j : j + 1]) * query))
    for j, (both, queries) in enumerate(scores):
        res = dot(both, solutions[j])
        at = slice(j * DV, (j + 1) * DV)
        inside[:, at] = res[:, DK:]
        eff[:, at] = (queries - res[:, :DK]).astype(BF16)

    def gates(first, stop):
        for n in range(first, stop, TILE):
            raw_gate = dot(ext[HALO:], vz[:, n : n + TILE])
            gains = jnp.concatenate([gain[...]] * (TILE // DV), 1)
            gate[:, n : n + TILE] = silu(raw_gate) * gains

    tail_copies[1].wait()
    gates(0, gate.shape[1] // 2)

    for j in range(GROUP):

        @pl.when(j != me)
        def _(j=j):
            remote(maps.at[j], land.at[j], send1.at[j], recv1.at[j], base + j, z).wait_recv()

    m = [land[j].astype(F32) for j in range(GROUP)]
    p01, p23, p45, p67 = (compose(m[2 * k + 1], m[2 * k]) for k in range(4))
    p03, p47 = compose(p23, p01), compose(p67, p45)
    total[...] = compose(p47, p03).astype(BF16)

    def first_total(other):
        return remote(
            total.at[:, pl.ds(DK, DV)], land2.at[0, :, pl.ds(DK, DV)], send2.at[other], recv2.at[0],
            other * GROUP + me, z,
        )

    for other in range(1, groups):

        @pl.when((g > 0) & (g < other))
        def _(other=other):
            remote(total, land2.at[g], send2.at[other], recv2.at[g], other * GROUP + me, z).start()

        @pl.when(g == 0)
        def _(other=other):
            first_total(other).start()

    p05 = compose(p45, p03)
    pref[0] = jnp.zeros((DK, DK + DV), F32)
    for j, item in enumerate((m[0], p01, compose(m[2], p01), p03, compose(m[4], p03), p05, compose(m[6], p05))):
        pref[j + 1] = item

    state[...] = jnp.zeros_like(state)
    gates(gate.shape[1] // 2, gate.shape[1])
    tail_copies[2].wait()

    @pl.when(g > 0)
    def _():
        first_total(0).wait_recv()
        state[...] = land2[0, :, DK:].astype(F32)

    for other in range(1, groups - 1):

        @pl.when(other < g)
        def _(other=other):
            remote(total, land2.at[other], send2.at[0], recv2.at[other], other * GROUP + me, z).wait_recv()
            now = state[...]
            step = land2[other]
            state[...] = now + step[:, DK:].astype(F32) + dot(step[:, :DK], now.astype(BF16))

    now = state[...]
    low = now.astype(BF16)

    def enter(j):
        item = pref[j]
        sbuf[j] = (now + item[:, DK:] + dot(item[:, :DK].astype(BF16), low)).astype(BF16)

    def entered(peer):
        return remote(sbuf.at[peer], s_in.at[me], send3.at[peer], recv3.at[me], base + peer, z)

    for batch in ((4, 5, 3, 6), (2, 7, 1, 0)):
        peers = [lax.rem(me + d, GROUP) for d in batch]
        for peer in peers:
            enter(peer)
        for d, peer in zip(batch, peers):
            if d:
                entered(peer).start()
    s_in[me] = sbuf[me]

    for batch in ((0, 1, 7), (2, 6), (3, 5, 4)):
        members = [lax.rem(me + d, GROUP) for d in batch]
        for d, j in zip(batch, members):
            if d:
                remote(sbuf.at[j], s_in.at[j], send3.at[j], recv3.at[j], base + j, z).wait_recv()
        cores = []
        for j in members:
            at = pl.ds(pl.multiple_of(j * DV, DV), DV)
            cores.append((at, inside[:, at] + dot(eff[:, at], s_in[j])))
        for at, core in cores:
            scale = lax.rsqrt(jnp.mean(core * core, -1, keepdims=True) + 1e-06)
            gated[:, at] = (core * scale * gate[:, at]).astype(BF16)

    width = part.shape[2] // 2
    lo, hi = slice(0, width), slice(width, 2 * width)
    relays = (
        remote(part.at[far, :, lo], relay.at[0], rsend.at[0], rrecv.at[0], c, up),
        remote(part.at[far, :, hi], relay.at[1], rsend.at[1], rrecv.at[1], c, down),
    )
    direct = (
        remote(part.at[down, :, lo], reduced.at[1, :, lo], dsend.at[0], drecv.at[0], c, down),
        remote(part.at[up, :, hi], reduced.at[0, :, hi], dsend.at[1], drecv.at[1], c, up),
    )
    summed = (
        remote(sums.at[0], reduced.at[0, :, lo], dsend.at[2], drecv.at[2], c, up),
        remote(sums.at[1], reduced.at[1, :, hi], dsend.at[3], drecv.at[3], c, down),
    )
    for k in range(2):
        for n in range(k * width, (k + 1) * width, TILE):
            tile = dot(gated[...], vo[:, n : n + TILE]).astype(BF16)
            part[:, :, n : n + TILE] = tile.reshape(part.shape[0], part.shape[1], TILE)
        relays[k].start()
        direct[k].start()
    for k, (peer, side) in enumerate(((up, lo), (down, hi))):
        relays[k].wait_recv()
        sums[k] = (part[peer, :, side].astype(F32) + relay[k].astype(F32)).astype(BF16)
        summed[k].start()
    for copy in direct + summed:
        copy.wait_recv()
    out[...] = (part[z].astype(F32) + reduced[0].astype(F32) + reduced[1].astype(F32)).astype(BF16)

    @pl.when(c < ctx - 1)
    def _():
        halo(c + 1).wait_send()

    for j in range(GROUP):

        @pl.when(j != me)
        def _(j=j):
            remote(maps.at[j], land.at[me], send1.at[j], recv1.at[me], base + j, z).wait_send()
            remote(sbuf.at[j], s_in.at[me], send3.at[j], recv3.at[me], base + j, z).wait_send()

    for other in range(1, groups):

        @pl.when((g > 0) & (g < other))
        def _(other=other):
            remote(total, land2.at[g], send2.at[other], recv2.at[g], other * GROUP + me, z).wait_send()

        @pl.when(g == 0)
        def _(other=other):
            first_total(other).wait_send()

    for copy in relays + direct + summed:
        copy.wait_send()


def local(
    activations, w_q, w_k, w_v, w_z, w_a, w_b, conv_q, conv_k, conv_v, a_log, dt_bias, norm_gain, w_o
):
    rows, depth = activations.shape
    heads = a_log.shape[0]
    groups = lax.axis_size("ctx") // GROUP
    parts = lax.axis_size("head")
    keys, values, wide = w_q.shape[1], w_v.shape[1], w_o.shape[1]
    hbm = pl.BlockSpec(memory_space=pl.ANY)
    vmem = pl.BlockSpec(memory_space=pltpu.VMEM)
    dma = pltpu.SemaphoreType.DMA
    piece = rows // parts
    return pl.pallas_call(
        functools.partial(kernel, groups),
        in_specs=[hbm] * 5 + [vmem] * 8 + [hbm],
        out_specs=vmem,
        out_shape=pltpu.VMEM((piece, wide), BF16),
        scratch_shapes=[
            pltpu.VMEM((HALO + rows, depth), BF16),
            pltpu.VMEM(w_q.shape, BF16),
            pltpu.VMEM(w_k.shape, BF16),
            pltpu.VMEM(w_v.shape, BF16),
            pltpu.VMEM(w_z.shape, BF16),
            pltpu.VMEM(w_o.shape, BF16),
            pltpu.VMEM((HALO + rows, 2 * keys + values), F32),
            pltpu.VMEM((rows, 128), F32),
            pltpu.VMEM((heads, rows), F32),
            pltpu.VMEM((rows, keys), BF16),
            pltpu.VMEM((heads, rows, DK + DV), BF16),
            pltpu.VMEM((rows, values), F32),
            pltpu.VMEM((rows, heads * DK), BF16),
            pltpu.VMEM((rows, values), F32),
            pltpu.VMEM((rows, values), BF16),
            pltpu.VMEM((heads, DK, DK + DV), BF16),
            pltpu.VMEM((GROUP, DK, DK + DV), BF16),
            pltpu.VMEM((DK, DK + DV), BF16),
            pltpu.VMEM((groups, DK, DK + DV), BF16),
            pltpu.VMEM((GROUP, DK, DK + DV), F32),
            pltpu.VMEM((DK, DV), F32),
            pltpu.VMEM((GROUP, DK, DV), BF16),
            pltpu.VMEM((GROUP, DK, DV), BF16),
            pltpu.VMEM((parts, piece, wide), BF16),
            pltpu.VMEM((2, piece, wide // 2), BF16),
            pltpu.VMEM((2, piece, wide // 2), BF16),
            pltpu.VMEM((2, piece, wide), BF16),
            dma((4 + 2 * STEPS,)),
            dma,
            dma,
            dma((GROUP,)),
            dma((GROUP,)),
            dma((groups,)),
            dma((groups,)),
            dma((GROUP,)),
            dma((GROUP,)),
            dma((2,)),
            dma((2,)),
            dma((4,)),
            dma((4,)),
        ],
        compiler_params=pltpu.CompilerParams(
            collective_id=0, has_side_effects=True, vmem_limit_bytes=VMEM_LIMIT
        ),
        name="gated_delta_layer",
    )(
        activations, w_q, w_k, w_v, w_z, jnp.transpose(w_a), jnp.transpose(w_b), conv_q, conv_k, conv_v,
        a_log.reshape(1, -1), dt_bias.reshape(1, -1), norm_gain.reshape(1, -1), w_o,
    )


def solution(mesh):
    in_specs = (
        P("ctx", None),
        P(None, "head"),
        P(None, "head"),
        P(None, "head"),
        P(None, "head"),
        P(None, "head"),
        P(None, "head"),
        P(None, "head"),
        P(None, "head"),
        P(None, "head"),
        P("head"),
        P("head"),
        P(),
        P("head", None),
    )
    out_specs = P(("ctx", "head"), None)
    return jax.shard_map(local, mesh=mesh, in_specs=in_specs, out_specs=out_specs, check_vma=False)
```

```python
import functools
import math

import jax
import jax.numpy as jnp
from jax import lax
from jax.experimental import pallas as pl
from jax.experimental.pallas import tpu as pltpu
from jax.sharding import PartitionSpec as P

DK = 128
DV = 128
KERNEL = 4
HALO = 16
GROUP = 8
STEPS = 2
TILE = 256
MESH = pl.DeviceIdType.MESH
F32 = jnp.float32
BF16 = jnp.bfloat16
VMEM_LIMIT = 56 * 1024 * 1024
HIGHEST = lax.Precision.HIGHEST
NN = ((1,), (0,))
NT = ((1,), (1,))


def dot(a, b, dims=NN, precision=None):
    return lax.dot_general(a, b, (dims, ((), ())), preferred_element_type=F32, precision=precision)


def remote(src, dst, send, recv, ctx, head):
    return pltpu.make_async_remote_copy(
        src_ref=src, dst_ref=dst, send_sem=send, recv_sem=recv, device_id=(ctx, head), device_id_type=MESH
    )


def silu(x):
    return x / (1.0 + jnp.exp(-x))


def unit(feature, scale):
    norm = jnp.sum(feature * feature, -1, keepdims=True) + 1e-06
    return feature * (lax.rsqrt(norm) * scale)


def column(row):
    n = row.shape[1]
    same = lax.broadcasted_iota(jnp.int32, (n, n), 0) == lax.broadcasted_iota(jnp.int32, (n, n), 1)
    return jnp.sum(jnp.where(same, jnp.broadcast_to(row, (n, n)), 0.0), 1, keepdims=True)


def each(a, b):
    n = a.shape[0]
    return jnp.concatenate([dot(a[:, :n], b[:, :n]), dot(a[:, n:], b[:, n:])], 1)


def invert(blocks, found):
    n = blocks[0].shape[0]
    row_at = lax.broadcasted_iota(jnp.int32, (n, 2 * n), 0)
    col_at = lax.broadcasted_iota(jnp.int32, (n, 2 * n), 1)
    differ = row_at ^ (col_at & (n - 1))
    one = jnp.where(differ == 0, 1.0, 0.0).astype(BF16)
    inverses = None
    width = 1
    while width < n:
        mask = jnp.where((differ >= width) & (differ < 2 * width), 1.0, 0.0).astype(BF16)
        lows = [block * mask for block in blocks]
        if inverses is None:
            inverses = [one - low for low in lows]
        else:
            right = [each(low, inv).astype(BF16) for low, inv in zip(lows, inverses)]
            yield
            left = [each(inv, r).astype(BF16) for inv, r in zip(inverses, right)]
            inverses = [inv - l for inv, l in zip(inverses, left)]
            yield
        width *= 2
    found.extend(inverses)


def compose(later, earlier):
    return later + earlier + dot(later[:, :DK].astype(BF16), earlier.astype(BF16))


def kernel(
    groups, act, w_q, w_k, w_v, w_z, w_at, w_bt, cq, ck, cv, a_log, dt_bias, gain, w_o,
    out,
    ext, vq, vk, vv, vz, vo, pad, colt, rowt, keyb, solutions, inside, eff, gate, gated,
    maps, land, total, land2, pref, state, sbuf, s_in,
    part, relay, sums, reduced,
    lsem, hsend, hrecv, send1, recv1, send2, recv2, send3, recv3, rsend, rrecv, dsend, drecv,
):
    c = lax.axis_index("ctx")
    z = lax.axis_index("head")
    ctx = groups * GROUP
    g = c // GROUP
    me = lax.rem(c, GROUP)
    base = g * GROUP
    up, down, far = lax.rem(z + 1, 4), lax.rem(z + 3, 4), lax.rem(z + 2, 4)
    rows = act.shape[0]
    half = rows // 2
    heads = maps.shape[0]
    per = heads // STEPS
    kw, vw = w_q.shape[1] // STEPS, w_v.shape[1] // STEPS
    keys = w_q.shape[1]

    def fetch(step):
        ks, vs = pl.ds(step * kw, kw), pl.ds(step * vw, vw)
        return [
            pltpu.make_async_copy(w_k.at[:, ks], vk.at[:, ks], lsem.at[1 + 2 * step]),
            pltpu.make_async_copy(w_v.at[:, vs], vv.at[:, vs], lsem.at[2 + 2 * step]),
        ]

    own = pltpu.make_async_copy(act, ext.at[pl.ds(HALO, rows)], lsem.at[0])
    last = 1 + 2 * STEPS
    tail_copies = [
        pltpu.make_async_copy(w_q, vq, lsem.at[last]),
        pltpu.make_async_copy(w_z, vz, lsem.at[last + 1]),
        pltpu.make_async_copy(w_o, vo, lsem.at[last + 2]),
    ]
    own.start()
    for copy in fetch(0) + fetch(1):
        copy.start()

    barrier = pltpu.get_barrier_semaphore()

    def greet(ctx_at, head_at):
        pl.semaphore_signal(barrier, inc=1, device_id=(ctx_at, head_at), device_id_type=MESH)

    for d in range(1, GROUP):
        greet(base + lax.rem(me + d, GROUP), z)
    for d in range(1, groups):
        greet(lax.rem(g + d, groups) * GROUP + me, z)
    greet(c, up)
    greet(c, down)

    @pl.when(me == 0)
    def _():
        greet(lax.rem(c + ctx - 1, ctx), z)

    pl.semaphore_wait(barrier, GROUP - 1 + groups - 1 + 2 + jnp.where(me == GROUP - 1, 1, 0))

    def halo(to):
        return remote(
            act.at[pl.ds(rows - HALO, HALO)], ext.at[pl.ds(0, HALO)], hsend, hrecv, to, z
        )

    @pl.when(c < ctx - 1)
    def _():
        halo(c + 1).start()

    @pl.when(c == 0)
    def _():
        ext[0:HALO] = jnp.zeros((HALO, ext.shape[1]), BF16)

    def project(weights, n, to, first, count):
        out_n = dot(ext[first : first + count], weights[:, n : n + TILE])
        pad[first : first + count, to + n : to + n + TILE] = out_n.astype(BF16).astype(F32)

    def projections(step, first, count):
        todo = []
        for weights, width, to in ((vk, kw, keys), (vv, vw, 2 * keys)):
            for n in range(step * width, (step + 1) * width, TILE):
                todo.append(functools.partial(project, weights, n, to, first, count))
        return todo

    own.wait()
    tokens = ext[HALO:]
    beta = 1.0 / (1.0 + jnp.exp(-dot(w_bt[...], tokens, NT)))
    raw = dot(w_at[...], tokens, NT) + column(dt_bias[...])
    soft = jnp.maximum(raw, 0.0) + jnp.log1p(jnp.exp(-jnp.abs(raw)))
    logdecay = -jnp.exp(column(a_log[...])) * soft
    upto = (
        lax.broadcasted_iota(jnp.int32, (rows, rows), 0) <= lax.broadcasted_iota(jnp.int32, (rows, rows), 1)
    )
    cum = dot(logdecay, jnp.where(upto, 1.0, 0.0), NN, HIGHEST)
    rowt[...] = cum
    both = jnp.concatenate([cum, beta], 0)
    colt[...] = jnp.concatenate([both] * (128 // both.shape[0]), 0).T
    for copy in fetch(0):
        copy.wait()
    for copy in tail_copies:
        copy.start()
    for work in projections(0, HALO, rows):
        work()

    @pl.when(c > 0)
    def _():
        halo(c).wait_recv()

    for work in projections(0, 0, HALO):
        work()

    row_at = lax.broadcasted_iota(jnp.int32, (half, half), 0)
    col_at = lax.broadcasted_iota(jnp.int32, (half, half), 1)
    lower = row_at >= col_at
    eye = jnp.where(
        lax.broadcasted_iota(jnp.int32, (DK, DK), 0) == lax.broadcasted_iota(jnp.int32, (DK, DK), 1), 1.0, 0.0
    )

    def smooth(at, taps, taps_at):
        w = taps[:, taps_at : taps_at + DK]
        sum_ = w[KERNEL - 1 : KERNEL] * pad[HALO:, at : at + DK]
        for back in range(1, KERNEL):
            tap = w[KERNEL - 1 - back : KERNEL - back]
            sum_ = sum_ + tap * pad[HALO - back : HALO - back + rows, at : at + DK]
        return silu(sum_)

    def factors(j):
        col, row = colt[:, j : j + 1], rowt[j : j + 1, :]
        f11 = jnp.exp(jnp.where(lower, col[:half] - row[:, :half], -1e30))
        f22 = jnp.exp(jnp.where(lower, col[half:] - row[:, half:], -1e30))
        f21 = jnp.exp(col[half:] - row[:, :half])
        return f11, f22, f21

    def prepare(h, items):
        key = unit(smooth(keys + h * DK, ck, h * DK), 1.0)
        kb = key.astype(BF16)
        keyb[:, h * DK : (h + 1) * DK] = kb
        kk = dot(kb, kb, NT)
        key_t = key.T
        for j in range(2 * h, 2 * h + 2):
            value = smooth(2 * keys + j * DV, cv, j * DV)
            f11, f22, f21 = factors(j)
            b = colt[:, heads + j : heads + j + 1]
            row = rowt[j : j + 1, :]
            a11 = (b[:half] * kk[:half, :half] * f11).astype(BF16)
            a22 = (b[half:] * kk[half:, half:] * f22).astype(BF16)
            a21 = (b[half:] * kk[half:, :half] * f21).astype(BF16)
            final = row[:, rows - 1 : rows]
            carried = (key_t * jnp.exp(final - row)).astype(BF16)
            rhs = jnp.concatenate([key * (jnp.exp(colt[:, j : j + 1]) * b), value * b], 1).astype(BF16)
            items.append((j, jnp.concatenate([a11, a22], 1), a21, carried, rhs, final))

    def conclude(items, inverses):
        halves = [(inv[:, :half], inv[:, half:]) for inv in inverses]
        lows = [dot(item[2], x11).astype(BF16) for item, (x11, _) in zip(items, halves)]
        yield
        corners = [-dot(x22, low) for low, (_, x22) in zip(lows, halves)]
        wholes = [
            jnp.concatenate(
                [
                    jnp.concatenate([x11, jnp.zeros_like(x11)], 1),
                    jnp.concatenate([x21.astype(BF16), x22], 1),
                ],
                0,
            )
            for x21, (x11, x22) in zip(corners, halves)
        ]
        yield
        solved = [dot(whole, item[4]).astype(BF16) for item, whole in zip(items, wholes)]
        yield
        results = [dot(item[3], wu) for item, wu in zip(items, solved)]
        for (j, _, _, _, _, final), res, wu in zip(items, results, solved):
            first = (jnp.exp(final) - 1.0) * eye - res[:, :DK]
            maps[j] = jnp.concatenate([first, res[:, DK:]], 1).astype(BF16)
            solutions[j] = wu
        yield

    def owner(j):
        return 2 * (j % per) + j // per

    def owned(member):
        return member // 2 + per * lax.rem(member, 2)

    mine = owned(me)

    def dispatch(step):
        for j in range(step * per, (step + 1) * per):

            @pl.when(owner(j) != me)
            def _(j=j):
                remote(maps.at[j], land.at[me], send1.at[j], recv1.at[me], base + owner(j), z).start()

            @pl.when(owner(j) == me)
            def _(j=j):
                land[me] = maps[j]

    key_heads = kw // DK
    early, later = [], []
    for h in range(key_heads):
        prepare(h, early)
    for copy in fetch(1):
        copy.wait()
    for work in projections(1, 0, HALO + rows):
        work()
    for h in range(key_heads, 2 * key_heads):
        prepare(h, later)
    found = []
    for _ in invert([item[1] for item in early + later], found):
        pass
    for _ in conclude(early, found[:per]):
        pass
    dispatch(0)
    for _ in conclude(later, found[per:]):
        pass
    dispatch(1)

    tail_copies[0].wait()
    for n in range(0, keys, TILE):
        project(vq, n, 0, 0, HALO + rows)
    scores = []
    for h in range(keys // DK):
        query = unit(smooth(h * DK, cq, h * DK), 1.0 / math.sqrt(DK))
        qk = dot(query.astype(BF16), keyb[:, h * DK : (h + 1) * DK], NT)
        for j in range(2 * h, 2 * h + 2):
            f11, f22, f21 = factors(j)
            s1 = jnp.concatenate([qk[:half, :half] * f11, jnp.zeros((half, half), F32)], 1)
            s2 = jnp.concatenate([qk[half:, :half] * f21, qk[half:, half:] * f22], 1)
            both = jnp.concatenate([s1, s2], 0).astype(BF16)
            scores.append((both, jnp.exp(colt[:, j : j + 1]) * query))
    for j, (both, queries) in enumerate(scores):
        res = dot(both, solutions[j])
        at = slice(j * DV, (j + 1) * DV)
        inside[:, at] = res[:, DK:]
        eff[:, at] = (queries - res[:, :DK]).astype(BF16)

    def gates(first, stop):
        for n in range(first, stop, TILE):
            raw_gate = dot(ext[HALO:], vz[:, n : n + TILE])
            gains = jnp.concatenate([gain[...]] * (TILE // DV), 1)
            gate[:, n : n + TILE] = silu(raw_gate) * gains

    tail_copies[1].wait()
    gates(0, gate.shape[1] // 2)

    for j in range(GROUP):

        @pl.when(j != me)
        def _(j=j):
            remote(maps.at[j], land.at[j], send1.at[j], recv1.at[j], base + j, z).wait_recv()

    m = [land[j].astype(F32) for j in range(GROUP)]
    p01, p23, p45, p67 = (compose(m[2 * k + 1], m[2 * k]) for k in range(4))
    p03, p47 = compose(p23, p01), compose(p67, p45)
    total[...] = compose(p47, p03).astype(BF16)

    def first_total(other):
        return remote(
            total.at[:, pl.ds(DK, DV)], land2.at[0, :, pl.ds(DK, DV)], send2.at[other], recv2.at[0],
            other * GROUP + me, z,
        )

    for other in range(1, groups):

        @pl.when((g > 0) & (g < other))
        def _(other=other):
            remote(total, land2.at[g], send2.at[other], recv2.at[g], other * GROUP + me, z).start()

        @pl.when(g == 0)
        def _(other=other):
            first_total(other).start()

    p05 = compose(p45, p03)
    pref[0] = jnp.zeros((DK, DK + DV), F32)
    for j, item in enumerate((m[0], p01, compose(m[2], p01), p03, compose(m[4], p03), p05, compose(m[6], p05))):
        pref[j + 1] = item

    state[...] = jnp.zeros_like(state)
    gates(gate.shape[1] // 2, gate.shape[1])
    tail_copies[2].wait()

    @pl.when(g > 0)
    def _():
        first_total(0).wait_recv()
        state[...] = land2[0, :, DK:].astype(F32)

    for other in range(1, groups - 1):

        @pl.when(other < g)
        def _(other=other):
            remote(total, land2.at[other], send2.at[0], recv2.at[other], other * GROUP + me, z).wait_recv()
            now = state[...]
            step = land2[other]
            state[...] = now + step[:, DK:].astype(F32) + dot(step[:, :DK], now.astype(BF16))

    now = state[...]
    low = now.astype(BF16)

    def enter(j):
        item = pref[j]
        sbuf[j] = (now + item[:, DK:] + dot(item[:, :DK].astype(BF16), low)).astype(BF16)

    def entered(peer):
        return remote(sbuf.at[peer], s_in.at[mine], send3.at[peer], recv3.at[mine], base + peer, z)

    for batch in ((4, 5, 3, 6), (2, 7, 1, 0)):
        peers = [lax.rem(me + d, GROUP) for d in batch]
        for peer in peers:
            enter(peer)
        for d, peer in zip(batch, peers):
            if d:
                entered(peer).start()
    s_in[mine] = sbuf[me]

    for batch in ((0, 1, 7), (2, 6), (3, 5, 4)):
        members = [lax.rem(me + d, GROUP) for d in batch]
        cores = []
        for d, peer in zip(batch, members):
            if d:
                j = owned(peer)
                remote(sbuf.at[peer], s_in.at[j], send3.at[peer], recv3.at[j], base + peer, z).wait_recv()
        for j in map(owned, members):
            at = pl.ds(pl.multiple_of(j * DV, DV), DV)
            cores.append((at, inside[:, at] + dot(eff[:, at], s_in[j])))
        for at, core in cores:
            scale = lax.rsqrt(jnp.mean(core * core, -1, keepdims=True) + 1e-06)
            gated[:, at] = (core * scale * gate[:, at]).astype(BF16)

    width = part.shape[2] // 2
    lo, hi = slice(0, width), slice(width, 2 * width)
    relays = (
        remote(part.at[far, :, lo], relay.at[0], rsend.at[0], rrecv.at[0], c, up),
        remote(part.at[far, :, hi], relay.at[1], rsend.at[1], rrecv.at[1], c, down),
    )
    direct = (
        remote(part.at[down, :, lo], reduced.at[1, :, lo], dsend.at[0], drecv.at[0], c, down),
        remote(part.at[up, :, hi], reduced.at[0, :, hi], dsend.at[1], drecv.at[1], c, up),
    )
    summed = (
        remote(sums.at[0], reduced.at[0, :, lo], dsend.at[2], drecv.at[2], c, up),
        remote(sums.at[1], reduced.at[1, :, hi], dsend.at[3], drecv.at[3], c, down),
    )
    for k in range(2):
        for n in range(k * width, (k + 1) * width, TILE):
            tile = dot(gated[...], vo[:, n : n + TILE]).astype(BF16)
            part[:, :, n : n + TILE] = tile.reshape(part.shape[0], part.shape[1], TILE)
        relays[k].start()
        direct[k].start()
    for k, (peer, side) in enumerate(((up, lo), (down, hi))):
        relays[k].wait_recv()
        sums[k] = (part[peer, :, side].astype(F32) + relay[k].astype(F32)).astype(BF16)
        summed[k].start()
    @pl.when(c < ctx - 1)
    def _():
        halo(c + 1).wait_send()

    for j in range(GROUP):

        @pl.when(owner(j) != me)
        def _(j=j):
            remote(maps.at[j], land.at[me], send1.at[j], recv1.at[me], base + owner(j), z).wait_send()

        @pl.when(j != me)
        def _(j=j):
            entered(j).wait_send()

    for other in range(1, groups):

        @pl.when((g > 0) & (g < other))
        def _(other=other):
            remote(total, land2.at[g], send2.at[other], recv2.at[g], other * GROUP + me, z).wait_send()

        @pl.when(g == 0)
        def _(other=other):
            first_total(other).wait_send()

    for copy in direct + summed:
        copy.wait_recv()
    out[...] = (part[z].astype(F32) + reduced[0].astype(F32) + reduced[1].astype(F32)).astype(BF16)

    for copy in relays + direct + summed:
        copy.wait_send()


def local(
    activations, w_q, w_k, w_v, w_z, w_a, w_b, conv_q, conv_k, conv_v, a_log, dt_bias, norm_gain, w_o
):
    rows, depth = activations.shape
    heads = a_log.shape[0]
    groups = lax.axis_size("ctx") // GROUP
    parts = lax.axis_size("head")
    keys, values, wide = w_q.shape[1], w_v.shape[1], w_o.shape[1]
    hbm = pl.BlockSpec(memory_space=pl.ANY)
    vmem = pl.BlockSpec(memory_space=pltpu.VMEM)
    dma = pltpu.SemaphoreType.DMA
    piece = rows // parts
    return pl.pallas_call(
        functools.partial(kernel, groups),
        in_specs=[hbm] * 5 + [vmem] * 8 + [hbm],
        out_specs=vmem,
        out_shape=pltpu.VMEM((piece, wide), BF16),
        scratch_shapes=[
            pltpu.VMEM((HALO + rows, depth), BF16),
            pltpu.VMEM(w_q.shape, BF16),
            pltpu.VMEM(w_k.shape, BF16),
            pltpu.VMEM(w_v.shape, BF16),
            pltpu.VMEM(w_z.shape, BF16),
            pltpu.VMEM(w_o.shape, BF16),
            pltpu.VMEM((HALO + rows, 2 * keys + values), F32),
            pltpu.VMEM((rows, 128), F32),
            pltpu.VMEM((heads, rows), F32),
            pltpu.VMEM((rows, keys), BF16),
            pltpu.VMEM((heads, rows, DK + DV), BF16),
            pltpu.VMEM((rows, values), F32),
            pltpu.VMEM((rows, heads * DK), BF16),
            pltpu.VMEM((rows, values), F32),
            pltpu.VMEM((rows, values), BF16),
            pltpu.VMEM((heads, DK, DK + DV), BF16),
            pltpu.VMEM((GROUP, DK, DK + DV), BF16),
            pltpu.VMEM((DK, DK + DV), BF16),
            pltpu.VMEM((groups, DK, DK + DV), BF16),
            pltpu.VMEM((GROUP, DK, DK + DV), F32),
            pltpu.VMEM((DK, DV), F32),
            pltpu.VMEM((GROUP, DK, DV), BF16),
            pltpu.VMEM((GROUP, DK, DV), BF16),
            pltpu.VMEM((parts, piece, wide), BF16),
            pltpu.VMEM((2, piece, wide // 2), BF16),
            pltpu.VMEM((2, piece, wide // 2), BF16),
            pltpu.VMEM((2, piece, wide), BF16),
            dma((4 + 2 * STEPS,)),
            dma,
            dma,
            dma((GROUP,)),
            dma((GROUP,)),
            dma((groups,)),
            dma((groups,)),
            dma((GROUP,)),
            dma((GROUP,)),
            dma((2,)),
            dma((2,)),
            dma((4,)),
            dma((4,)),
        ],
        compiler_params=pltpu.CompilerParams(
            collective_id=0, has_side_effects=True, vmem_limit_bytes=VMEM_LIMIT
        ),
        name="gated_delta_layer",
    )(
        activations, w_q, w_k, w_v, w_z, jnp.transpose(w_a), jnp.transpose(w_b), conv_q, conv_k, conv_v,
        a_log.reshape(1, -1), dt_bias.reshape(1, -1), norm_gain.reshape(1, -1), w_o,
    )


def solution(mesh):
    in_specs = (
        P("ctx", None),
        P(None, "head"),
        P(None, "head"),
        P(None, "head"),
        P(None, "head"),
        P(None, "head"),
        P(None, "head"),
        P(None, "head"),
        P(None, "head"),
        P(None, "head"),
        P("head"),
        P("head"),
        P(),
        P("head", None),
    )
    out_specs = P(("ctx", "head"), None)
    return jax.shard_map(local, mesh=mesh, in_specs=in_specs, out_specs=out_specs, check_vma=False)
```

```python
import functools
import math

import jax
import jax.numpy as jnp
from jax import lax
from jax.experimental import pallas as pl
from jax.experimental.pallas import tpu as pltpu
from jax.sharding import PartitionSpec as P

DK = 128
DV = 128
KERNEL = 4
HALO = 16
GROUP = 8
STEPS = 2
TILE = 256
MESH = pl.DeviceIdType.MESH
F32 = jnp.float32
BF16 = jnp.bfloat16
VMEM_LIMIT = 56 * 1024 * 1024
HIGHEST = lax.Precision.HIGHEST
NN = ((1,), (0,))
NT = ((1,), (1,))


def dot(a, b, dims=NN, precision=None):
    return lax.dot_general(a, b, (dims, ((), ())), preferred_element_type=F32, precision=precision)


def remote(src, dst, send, recv, ctx, head):
    return pltpu.make_async_remote_copy(
        src_ref=src, dst_ref=dst, send_sem=send, recv_sem=recv, device_id=(ctx, head), device_id_type=MESH
    )


def silu(x):
    return x / (1.0 + jnp.exp(-x))


def unit(feature, scale):
    norm = jnp.sum(feature * feature, -1, keepdims=True) + 1e-06
    return feature * (lax.rsqrt(norm) * scale)


def column(row):
    n = row.shape[1]
    same = lax.broadcasted_iota(jnp.int32, (n, n), 0) == lax.broadcasted_iota(jnp.int32, (n, n), 1)
    return jnp.sum(jnp.where(same, jnp.broadcast_to(row, (n, n)), 0.0), 1, keepdims=True)


def each(a, b):
    n = a.shape[0]
    return jnp.concatenate([dot(a[:, :n], b[:, :n]), dot(a[:, n:], b[:, n:])], 1)


def invert(blocks, found):
    n = blocks[0].shape[0]
    row_at = lax.broadcasted_iota(jnp.int32, (n, 2 * n), 0)
    col_at = lax.broadcasted_iota(jnp.int32, (n, 2 * n), 1)
    differ = row_at ^ (col_at & (n - 1))
    one = jnp.where(differ == 0, 1.0, 0.0).astype(BF16)
    inverses = None
    width = 1
    while width < n:
        mask = jnp.where((differ >= width) & (differ < 2 * width), 1.0, 0.0).astype(BF16)
        lows = [block * mask for block in blocks]
        if inverses is None:
            inverses = [one - low for low in lows]
        else:
            right = [each(low, inv).astype(BF16) for low, inv in zip(lows, inverses)]
            yield
            left = [each(inv, r).astype(BF16) for inv, r in zip(inverses, right)]
            inverses = [inv - l for inv, l in zip(inverses, left)]
            yield
        width *= 2
    found.extend(inverses)


def compose(later, earlier):
    return later + earlier + dot(later[:, :DK].astype(BF16), earlier.astype(BF16))


def kernel(
    groups, act, w_q, w_k, w_v, w_z, w_at, w_bt, cq, ck, cv, a_log, dt_bias, gain, w_o,
    out,
    ext, vq, vk, vv, vz, vo, pad, colt, rowt, keyb, solutions, inside, eff, gate, gated,
    maps, land, total, land2, pref, state, sbuf, s_in,
    part, relay, sums, reduced,
    lsem, hsend, hrecv, send1, recv1, send2, recv2, send3, recv3, rsend, rrecv, dsend, drecv,
):
    c = lax.axis_index("ctx")
    z = lax.axis_index("head")
    ctx = groups * GROUP
    g = c // GROUP
    me = lax.rem(c, GROUP)
    base = g * GROUP
    up, down, far = lax.rem(z + 1, 4), lax.rem(z + 3, 4), lax.rem(z + 2, 4)
    rows = act.shape[0]
    half = rows // 2
    heads = maps.shape[0]
    per = heads // STEPS
    kw, vw = w_q.shape[1] // STEPS, w_v.shape[1] // STEPS
    keys = w_q.shape[1]

    def fetch(step):
        ks, vs = pl.ds(step * kw, kw), pl.ds(step * vw, vw)
        return [
            pltpu.make_async_copy(w_k.at[:, ks], vk.at[:, ks], lsem.at[1 + 2 * step]),
            pltpu.make_async_copy(w_v.at[:, vs], vv.at[:, vs], lsem.at[2 + 2 * step]),
        ]

    own = pltpu.make_async_copy(act, ext.at[pl.ds(HALO, rows)], lsem.at[0])
    last = 1 + 2 * STEPS
    tail_copies = [
        pltpu.make_async_copy(w_q, vq, lsem.at[last]),
        pltpu.make_async_copy(w_z, vz, lsem.at[last + 1]),
        pltpu.make_async_copy(w_o, vo, lsem.at[last + 2]),
    ]
    own.start()
    for copy in fetch(0) + fetch(1):
        copy.start()

    barrier = pltpu.get_barrier_semaphore()

    def greet(ctx_at, head_at):
        pl.semaphore_signal(barrier, inc=1, device_id=(ctx_at, head_at), device_id_type=MESH)

    for d in range(1, GROUP):
        greet(base + lax.rem(me + d, GROUP), z)
    for d in range(1, groups):
        greet(lax.rem(g + d, groups) * GROUP + me, z)
    greet(c, up)
    greet(c, down)

    @pl.when(me == 0)
    def _():
        greet(lax.rem(c + ctx - 1, ctx), z)

    pl.semaphore_wait(barrier, GROUP - 1 + groups - 1 + 2 + jnp.where(me == GROUP - 1, 1, 0))

    def halo(to):
        return remote(
            act.at[pl.ds(rows - HALO, HALO)], ext.at[pl.ds(0, HALO)], hsend, hrecv, to, z
        )

    @pl.when(c < ctx - 1)
    def _():
        halo(c + 1).start()

    @pl.when(c == 0)
    def _():
        ext[0:HALO] = jnp.zeros((HALO, ext.shape[1]), BF16)

    def project(weights, n, to, first, count):
        out_n = dot(ext[first : first + count], weights[:, n : n + TILE])
        pad[first : first + count, to + n : to + n + TILE] = out_n.astype(BF16).astype(F32)

    def projections(step, first, count):
        todo = []
        for weights, width, to in ((vk, kw, keys), (vv, vw, 2 * keys)):
            for n in range(step * width, (step + 1) * width, TILE):
                todo.append(functools.partial(project, weights, n, to, first, count))
        return todo

    own.wait()
    tokens = ext[HALO:]
    beta = 1.0 / (1.0 + jnp.exp(-dot(w_bt[...], tokens, NT)))
    raw = dot(w_at[...], tokens, NT) + column(dt_bias[...])
    soft = jnp.maximum(raw, 0.0) + jnp.log1p(jnp.exp(-jnp.abs(raw)))
    logdecay = -jnp.exp(column(a_log[...])) * soft
    upto = (
        lax.broadcasted_iota(jnp.int32, (rows, rows), 0) <= lax.broadcasted_iota(jnp.int32, (rows, rows), 1)
    )
    cum = dot(logdecay, jnp.where(upto, 1.0, 0.0), NN, HIGHEST)
    rowt[...] = cum
    both = jnp.concatenate([cum, beta], 0)
    colt[...] = jnp.concatenate([both] * (128 // both.shape[0]), 0).T
    for copy in fetch(0):
        copy.wait()
    for copy in tail_copies:
        copy.start()
    for work in projections(0, HALO, rows):
        work()

    @pl.when(c > 0)
    def _():
        halo(c).wait_recv()

    for work in projections(0, 0, HALO):
        work()

    row_at = lax.broadcasted_iota(jnp.int32, (half, half), 0)
    col_at = lax.broadcasted_iota(jnp.int32, (half, half), 1)
    lower = row_at >= col_at
    eye = jnp.where(
        lax.broadcasted_iota(jnp.int32, (DK, DK), 0) == lax.broadcasted_iota(jnp.int32, (DK, DK), 1), 1.0, 0.0
    )

    def smooth(at, taps, taps_at):
        w = taps[:, taps_at : taps_at + DK]
        sum_ = w[KERNEL - 1 : KERNEL] * pad[HALO:, at : at + DK]
        for back in range(1, KERNEL):
            tap = w[KERNEL - 1 - back : KERNEL - back]
            sum_ = sum_ + tap * pad[HALO - back : HALO - back + rows, at : at + DK]
        return silu(sum_)

    def factors(j):
        col, row = colt[:, j : j + 1], rowt[j : j + 1, :]
        f11 = jnp.exp(jnp.where(lower, col[:half] - row[:, :half], -1e30))
        f22 = jnp.exp(jnp.where(lower, col[half:] - row[:, half:], -1e30))
        f21 = jnp.exp(col[half:] - row[:, :half])
        return f11, f22, f21

    def prepare(h, items):
        key = unit(smooth(keys + h * DK, ck, h * DK), 1.0)
        kb = key.astype(BF16)
        keyb[:, h * DK : (h + 1) * DK] = kb
        kk = dot(kb, kb, NT)
        key_t = key.T
        for j in range(2 * h, 2 * h + 2):
            value = smooth(2 * keys + j * DV, cv, j * DV)
            f11, f22, f21 = factors(j)
            b = colt[:, heads + j : heads + j + 1]
            row = rowt[j : j + 1, :]
            a11 = (b[:half] * kk[:half, :half] * f11).astype(BF16)
            a22 = (b[half:] * kk[half:, half:] * f22).astype(BF16)
            a21 = (b[half:] * kk[half:, :half] * f21).astype(BF16)
            final = row[:, rows - 1 : rows]
            carried = (key_t * jnp.exp(final - row)).astype(BF16)
            rhs = jnp.concatenate([key * (jnp.exp(colt[:, j : j + 1]) * b), value * b], 1).astype(BF16)
            items.append((j, jnp.concatenate([a11, a22], 1), a21, carried, rhs, final))

    def conclude(items, inverses):
        halves = [(inv[:, :half], inv[:, half:]) for inv in inverses]
        lows = [dot(item[2], x11).astype(BF16) for item, (x11, _) in zip(items, halves)]
        yield
        corners = [-dot(x22, low) for low, (_, x22) in zip(lows, halves)]
        wholes = [
            jnp.concatenate(
                [
                    jnp.concatenate([x11, jnp.zeros_like(x11)], 1),
                    jnp.concatenate([x21.astype(BF16), x22], 1),
                ],
                0,
            )
            for x21, (x11, x22) in zip(corners, halves)
        ]
        yield
        solved = [dot(whole, item[4]).astype(BF16) for item, whole in zip(items, wholes)]
        yield
        results = [dot(item[3], wu) for item, wu in zip(items, solved)]
        for (j, _, _, _, _, final), res, wu in zip(items, results, solved):
            first = (jnp.exp(final) - 1.0) * eye - res[:, :DK]
            maps[j] = jnp.concatenate([first, res[:, DK:]], 1).astype(BF16)
            solutions[j] = wu
        yield

    def owner(j):
        return 2 * (j % per) + j // per

    def owned(member):
        return member // 2 + per * lax.rem(member, 2)

    mine = owned(me)

    def dispatch(step):
        for j in range(step * per, (step + 1) * per):

            @pl.when(owner(j) != me)
            def _(j=j):
                remote(maps.at[j], land.at[me], send1.at[j], recv1.at[me], base + owner(j), z).start()

            @pl.when(owner(j) == me)
            def _(j=j):
                land[me] = maps[j]

    key_heads = kw // DK
    early, later = [], []
    for h in range(key_heads):
        prepare(h, early)
    for copy in fetch(1):
        copy.wait()
    for work in projections(1, 0, HALO + rows):
        work()
    for h in range(key_heads, 2 * key_heads):
        prepare(h, later)
    found = []
    for _ in invert([item[1] for item in early + later], found):
        pass
    for _ in conclude(early, found[:per]):
        pass
    dispatch(0)
    for _ in conclude(later, found[per:]):
        pass
    dispatch(1)

    tail_copies[0].wait()
    for n in range(0, keys, TILE):
        project(vq, n, 0, 0, HALO + rows)
    scores = []
    for h in range(keys // DK):
        query = unit(smooth(h * DK, cq, h * DK), 1.0 / math.sqrt(DK))
        qk = dot(query.astype(BF16), keyb[:, h * DK : (h + 1) * DK], NT)
        for j in range(2 * h, 2 * h + 2):
            f11, f22, f21 = factors(j)
            s1 = jnp.concatenate([qk[:half, :half] * f11, jnp.zeros((half, half), F32)], 1)
            s2 = jnp.concatenate([qk[half:, :half] * f21, qk[half:, half:] * f22], 1)
            both = jnp.concatenate([s1, s2], 0).astype(BF16)
            scores.append((both, jnp.exp(colt[:, j : j + 1]) * query))
    for j, (both, queries) in enumerate(scores):
        res = dot(both, solutions[j])
        at = slice(j * DV, (j + 1) * DV)
        inside[:, at] = res[:, DK:]
        eff[:, at] = (queries - res[:, :DK]).astype(BF16)

    def gates(first, stop):
        for n in range(first, stop, TILE):
            raw_gate = dot(ext[HALO:], vz[:, n : n + TILE])
            gains = jnp.concatenate([gain[...]] * (TILE // DV), 1)
            gate[:, n : n + TILE] = silu(raw_gate) * gains

    tail_copies[1].wait()
    gates(0, gate.shape[1] // 2)

    for j in range(GROUP):

        @pl.when(j != me)
        def _(j=j):
            remote(maps.at[j], land.at[j], send1.at[j], recv1.at[j], base + j, z).wait_recv()

    m = [land[j].astype(F32) for j in range(GROUP)]
    p01, p23, p45, p67 = (compose(m[2 * k + 1], m[2 * k]) for k in range(4))
    p03, p47 = compose(p23, p01), compose(p67, p45)
    total[...] = compose(p47, p03).astype(BF16)

    def first_total(other):
        return remote(
            total.at[:, pl.ds(DK, DV)], land2.at[0, :, pl.ds(DK, DV)], send2.at[other], recv2.at[0],
            other * GROUP + me, z,
        )

    for other in range(1, groups):

        @pl.when((g > 0) & (g < other))
        def _(other=other):
            remote(total, land2.at[g], send2.at[other], recv2.at[g], other * GROUP + me, z).start()

        @pl.when(g == 0)
        def _(other=other):
            first_total(other).start()

    p05 = compose(p45, p03)
    pref[0] = jnp.zeros((DK, DK + DV), F32)
    for j, item in enumerate((m[0], p01, compose(m[2], p01), p03, compose(m[4], p03), p05, compose(m[6], p05))):
        pref[j + 1] = item

    state[...] = jnp.zeros_like(state)
    gates(gate.shape[1] // 2, gate.shape[1])
    tail_copies[2].wait()

    @pl.when(g > 0)
    def _():
        first_total(0).wait_recv()
        state[...] = land2[0, :, DK:].astype(F32)

    for other in range(1, groups - 1):

        @pl.when(other < g)
        def _(other=other):
            remote(total, land2.at[other], send2.at[0], recv2.at[other], other * GROUP + me, z).wait_recv()
            now = state[...]
            step = land2[other]
            state[...] = now + step[:, DK:].astype(F32) + dot(step[:, :DK], now.astype(BF16))

    now = state[...]
    low = now.astype(BF16)

    def enter(j):
        item = pref[j]
        sbuf[j] = (now + item[:, DK:] + dot(item[:, :DK].astype(BF16), low)).astype(BF16)

    def entered(peer):
        return remote(sbuf.at[peer], s_in.at[mine], send3.at[peer], recv3.at[mine], base + peer, z)

    for batch in ((4, 5, 3, 6), (2, 7, 1, 0)):
        peers = [lax.rem(me + d, GROUP) for d in batch]
        for peer in peers:
            enter(peer)
        for d, peer in zip(batch, peers):
            if d:
                entered(peer).start()
    s_in[mine] = sbuf[me]

    for batch in ((0, 1, 7), (2, 6), (3, 5, 4)):
        members = [lax.rem(me + d, GROUP) for d in batch]
        cores = []
        for d, peer in zip(batch, members):
            if d:
                j = owned(peer)
                remote(sbuf.at[peer], s_in.at[j], send3.at[peer], recv3.at[j], base + peer, z).wait_recv()
        for j in map(owned, members):
            at = pl.ds(pl.multiple_of(j * DV, DV), DV)
            cores.append((at, inside[:, at] + dot(eff[:, at], s_in[j])))
        for at, core in cores:
            scale = lax.rsqrt(jnp.mean(core * core, -1, keepdims=True) + 1e-06)
            gated[:, at] = (core * scale * gate[:, at]).astype(BF16)

    width = part.shape[2] // 2
    lo, hi = slice(0, width), slice(width, 2 * width)
    relays = (
        remote(part.at[far, :, lo], relay.at[0], rsend.at[0], rrecv.at[0], c, up),
        remote(part.at[far, :, hi], relay.at[1], rsend.at[1], rrecv.at[1], c, down),
    )
    direct = (
        remote(part.at[down, :, lo], reduced.at[1, :, lo], dsend.at[0], drecv.at[0], c, down),
        remote(part.at[up, :, hi], reduced.at[0, :, hi], dsend.at[1], drecv.at[1], c, up),
    )
    summed = (
        remote(sums.at[0], reduced.at[0, :, lo], dsend.at[2], drecv.at[2], c, up),
        remote(sums.at[1], reduced.at[1, :, hi], dsend.at[3], drecv.at[3], c, down),
    )
    for k in range(2):
        for n in range(k * width, (k + 1) * width, TILE):
            tile = dot(gated[...], vo[:, n : n + TILE]).astype(BF16)
            part[:, :, n : n + TILE] = tile.reshape(part.shape[0], part.shape[1], TILE)
        relays[k].start()
        direct[k].start()
    for k, (peer, side) in enumerate(((up, lo), (down, hi))):
        relays[k].wait_recv()
        sums[k] = (part[peer, :, side].astype(F32) + relay[k].astype(F32)).astype(BF16)
        summed[k].start()
    @pl.when(c < ctx - 1)
    def _():
        halo(c + 1).wait_send()

    for j in range(GROUP):

        @pl.when(owner(j) != me)
        def _(j=j):
            remote(maps.at[j], land.at[me], send1.at[j], recv1.at[me], base + owner(j), z).wait_send()

        @pl.when(j != me)
        def _(j=j):
            entered(j).wait_send()

    for other in range(1, groups):

        @pl.when((g > 0) & (g < other))
        def _(other=other):
            remote(total, land2.at[g], send2.at[other], recv2.at[g], other * GROUP + me, z).wait_send()

        @pl.when(g == 0)
        def _(other=other):
            first_total(other).wait_send()

    piece = out.shape[0]
    tops = (slice(0, piece), slice(piece, 2 * piece))
    for k, side in enumerate((lo, hi)):
        direct[k].wait_recv()
        inside[tops[k]] = part[z, :, side].astype(F32) + reduced[1 - k, :, side].astype(F32)
    for k, side in enumerate((lo, hi)):
        summed[k].wait_recv()
        out[:, side] = (inside[tops[k]] + reduced[k, :, side].astype(F32)).astype(BF16)

    for copy in relays + direct + summed:
        copy.wait_send()


def local(
    activations, w_q, w_k, w_v, w_z, w_a, w_b, conv_q, conv_k, conv_v, a_log, dt_bias, norm_gain, w_o
):
    rows, depth = activations.shape
    heads = a_log.shape[0]
    groups = lax.axis_size("ctx") // GROUP
    parts = lax.axis_size("head")
    keys, values, wide = w_q.shape[1], w_v.shape[1], w_o.shape[1]
    hbm = pl.BlockSpec(memory_space=pl.ANY)
    vmem = pl.BlockSpec(memory_space=pltpu.VMEM)
    dma = pltpu.SemaphoreType.DMA
    piece = rows // parts
    return pl.pallas_call(
        functools.partial(kernel, groups),
        in_specs=[hbm] * 5 + [vmem] * 8 + [hbm],
        out_specs=vmem,
        out_shape=pltpu.VMEM((piece, wide), BF16),
        scratch_shapes=[
            pltpu.VMEM((HALO + rows, depth), BF16),
            pltpu.VMEM(w_q.shape, BF16),
            pltpu.VMEM(w_k.shape, BF16),
            pltpu.VMEM(w_v.shape, BF16),
            pltpu.VMEM(w_z.shape, BF16),
            pltpu.VMEM(w_o.shape, BF16),
            pltpu.VMEM((HALO + rows, 2 * keys + values), F32),
            pltpu.VMEM((rows, 128), F32),
            pltpu.VMEM((heads, rows), F32),
            pltpu.VMEM((rows, keys), BF16),
            pltpu.VMEM((heads, rows, DK + DV), BF16),
            pltpu.VMEM((rows, values), F32),
            pltpu.VMEM((rows, heads * DK), BF16),
            pltpu.VMEM((rows, values), F32),
            pltpu.VMEM((rows, values), BF16),
            pltpu.VMEM((heads, DK, DK + DV), BF16),
            pltpu.VMEM((GROUP, DK, DK + DV), BF16),
            pltpu.VMEM((DK, DK + DV), BF16),
            pltpu.VMEM((groups, DK, DK + DV), BF16),
            pltpu.VMEM((GROUP, DK, DK + DV), F32),
            pltpu.VMEM((DK, DV), F32),
            pltpu.VMEM((GROUP, DK, DV), BF16),
            pltpu.VMEM((GROUP, DK, DV), BF16),
            pltpu.VMEM((parts, piece, wide), BF16),
            pltpu.VMEM((2, piece, wide // 2), BF16),
            pltpu.VMEM((2, piece, wide // 2), BF16),
            pltpu.VMEM((2, piece, wide), BF16),
            dma((4 + 2 * STEPS,)),
            dma,
            dma,
            dma((GROUP,)),
            dma((GROUP,)),
            dma((groups,)),
            dma((groups,)),
            dma((GROUP,)),
            dma((GROUP,)),
            dma((2,)),
            dma((2,)),
            dma((4,)),
            dma((4,)),
        ],
        compiler_params=pltpu.CompilerParams(
            collective_id=0, has_side_effects=True, vmem_limit_bytes=VMEM_LIMIT
        ),
        name="gated_delta_layer",
    )(
        activations, w_q, w_k, w_v, w_z, jnp.transpose(w_a), jnp.transpose(w_b), conv_q, conv_k, conv_v,
        a_log.reshape(1, -1), dt_bias.reshape(1, -1), norm_gain.reshape(1, -1), w_o,
    )


def solution(mesh):
    in_specs = (
        P("ctx", None),
        P(None, "head"),
        P(None, "head"),
        P(None, "head"),
        P(None, "head"),
        P(None, "head"),
        P(None, "head"),
        P(None, "head"),
        P(None, "head"),
        P(None, "head"),
        P("head"),
        P("head"),
        P(),
        P("head", None),
    )
    out_specs = P(("ctx", "head"), None)
    return jax.shard_map(local, mesh=mesh, in_specs=in_specs, out_specs=out_specs, check_vma=False)
```
